256 devices in a mesh: ctx: 16 (over x_lo, y, core), grp: 16 (over x_hi, z).
Axes of the slice: x: 4 (x_hi: 2, x_lo: 2; x = x_hi * 2 + x_lo), y: 4, z: 8, core: 2. Of those that a mesh axis runs over, the one named last changes fastest.
Arguments:
- queries: bfloat16 [1024, 12288], P(('ctx', 'grp')), may hold values from -240 to 240
- latents: bfloat16 [16384, 512], P(('ctx', 'grp')), may hold values from -6 to 6
- key_rope: bfloat16 [16384, 64], P(('ctx', 'grp')), may hold values from -4 to 4
- key_up: bfloat16 [64, 128, 512], P('grp'), may hold values from -0.5 to 0.5
- value_up: bfloat16 [64, 512, 128], P('grp'), may hold values from -0.25 to 0.25
- pattern: int32 [8, 128], replicated, may hold values 0 or 1
- stripe: int32 [128], replicated, may hold values from 0 to 127, each once
Outputs:
- attended: bfloat16 [1024, 8192], P(('ctx', 'grp'))
The draws below stay inside these ranges and needn't reach their ends.
All inputs are finite; a program needn't handle non-finite values.
Results may differ from the reference program's by a relative error of at most 0.011.
Values may be sent and summed in bfloat16 or wider, within the bound.
No kernel may reach another device: no remote copies, remote signals or barrier semaphores. Data moves between devices by JAX's collectives and lax.ppermute only.
A program may use at most 128 MiB of HBM per device.

```python
import math
import jax
import jax.numpy as jnp
from jax import lax

L = 512
QN = 128
QR = 64
VD = 128
H = 64
BLOCK = 128
LENGTH = 16384
SPAN = 1024
NB = 128
CB = 8


def draw_key_rope(key, part):
    rope_values = jnp.clip(jax.random.normal(jax.random.fold_in(key, 11), (LENGTH, QR), jnp.float32), -4.0, 4.0)
    return rope_values.astype(jnp.bfloat16)


def draw_queries(key, part):
    values = jnp.clip(jax.random.normal(jax.random.fold_in(key, 3), (SPAN, H, QN + QR), jnp.float32), -6.0, 6.0)
    return values.reshape(SPAN, H * (QN + QR)).astype(jnp.bfloat16)


def place_ends(result, stream_key, smallest, largest):
    longest = result.shape.index(max(result.shape))
    spots = []
    for shift in (0, 1):
        where = [jax.random.randint(jax.random.fold_in(stream_key, axis), (), 0, length) for axis, length in enumerate(result.shape)]
        where[longest] = (where[longest] + shift) % result.shape[longest]
        spots.append(tuple(where))
    return result.at[spots[0]].set(smallest).at[spots[1]].set(largest)


def block_levels(rng, extent, pieces, smallest, top_value):
    def one(dim, blocks):
        steps = jax.random.uniform(jax.random.fold_in(jax.random.fold_in(rng, 6), dim), (blocks,), jnp.float32, smallest / len(pieces), top_value / len(pieces))
        return jnp.repeat(jnp.exp(steps), extent[dim] // blocks).reshape((-1,) + (1,) * (len(extent) - dim - 1))

    factor_of = one(*pieces[0])
    for cut in pieces[1:]:
        factor_of = factor_of * one(*cut)
    return factor_of


def noise(own_key, dims, spread, most, shards=(), kind=jnp.bfloat16):
    result = spread * jax.random.normal(own_key, dims, jnp.float32)
    if shards:
        result = result * block_levels(own_key, dims, shards, -0.22, 0.18)
    return jnp.clip(result, -most, most).astype(kind)


def setup_inputs(seed: int = 0) -> dict:
    seeds = jax.random.split(jax.random.key(seed), 8)
    return {
        "queries": draw_queries(jax.random.fold_in(seeds[7], 71), 0),
        "latents": noise(seeds[1], (LENGTH, L), 1.0, 6.0, ((0, 256),)),
        "key_rope": draw_key_rope(jax.random.fold_in(seeds[7], 71), 0),
        "key_up": noise(seeds[3], (H, QN, L), QN ** -0.5, 0.5, ((0, 16),)),
        "value_up": noise(seeds[4], (H, L, VD), L ** -0.5, 0.25, ((0, 16),)),
        "pattern": place_ends((jax.random.randint(seeds[5], (CB, NB), 0, 2) < 1).astype(jnp.int32), jax.random.fold_in(seeds[5], 1), 0, 1),
        "stripe": jax.random.permutation(seeds[6], NB).astype(jnp.int32),
    }


def reference(queries, latents, key_rope, key_up, value_up, pattern, stripe):
    stored = jnp.arange(LENGTH, dtype=jnp.int32)
    key_block = stripe[stored // BLOCK]
    key_offset = stored % BLOCK
    query_ids = jnp.arange(SPAN, dtype=jnp.int32)
    query_pos = LENGTH - SPAN + query_ids
    query_block = query_pos // BLOCK
    query_offset = query_ids % BLOCK
    pattern_hit = pattern[(query_ids // BLOCK)[:, None], key_block[None, :]] == 1
    lower = query_block[:, None] > key_block[None, :]
    same_block = query_block[:, None] == key_block[None, :]
    allowed = lower & pattern_hit | same_block & (key_offset[None, :] <= query_offset[:, None])
    score_scale = 1.0 / math.sqrt(QN + QR)
    query_heads = queries.reshape(SPAN, H, QN + QR).transpose(1, 0, 2)

    def one_head(head_operands):
        query_head, up_key, up_value = head_operands
        absorbed = jnp.dot(query_head[:, :QN], up_key, preferred_element_type=jnp.float32).astype(jnp.bfloat16)
        scores = jnp.dot(absorbed, latents.T, preferred_element_type=jnp.float32)
        scores = scores + jnp.dot(query_head[:, QN:], key_rope.T, preferred_element_type=jnp.float32)
        scores = scores * score_scale
        masked = jnp.where(allowed, scores, -1e+30)
        highest = lax.optimization_barrier(jnp.max(masked, axis=1))
        weights = jnp.where(allowed, jnp.exp(scores - highest[:, None]), 0.0)
        denominator = lax.optimization_barrier(jnp.sum(weights, axis=1))
        numerator = jnp.dot(weights.astype(jnp.bfloat16), latents, preferred_element_type=jnp.float32)
        mixed = (numerator / denominator[:, None]).astype(jnp.bfloat16)
        return jnp.dot(mixed, up_value, preferred_element_type=jnp.float32).astype(jnp.bfloat16)
    outputs = lax.map(one_head, (query_heads, key_up, value_up))
    return outputs.transpose(1, 0, 2).reshape(SPAN, H * VD)
```

```python
import functools
import math

import jax
import jax.numpy as jnp
from jax import lax
from jax.experimental import pallas as pl
from jax.experimental.pallas import tpu as pltpu
from jax.sharding import Mesh
from jax.sharding import PartitionSpec as P

L = 512
QN = 128
QR = 64
QD = QN + QR
VD = 128
BLOCK = 128
HEADS = 4
NEG = -1e30
SCALE = 1.0 / math.sqrt(QD)
LOG2E = math.log2(math.e)

AXES = ("xl", "y", "core", "xh", "z")
CHIPS = ("xl", "y", "xh", "z")
XLN, YN, CN, XHN, ZN = 2, 4, 2, 2, 8
CELLS = XLN * YN
GRP = XHN * ZN
PER = 64
TOK = 4
ROWS = CELLS * GRP * TOK
SLOTS = 2 * CN * ZN
KEYS = SLOTS * PER
EXT = HEADS * VD + 128

QT = 256
KT = 512


def attend_kernel(q_ref, lat_ref, rope_ref, w_ref, thr_ref, off_ref, o_ref, kcat, vals, sco, stats):
    h = pl.program_id(0)
    for i in range(KEYS // KT):
        rows = pl.ds(i * KT, KT)
        kv = jnp.dot(lat_ref[rows, :], w_ref[0], preferred_element_type=jnp.float32)
        kv = kv.astype(jnp.bfloat16)
        kcat[rows, 0:QN] = kv[:, 0:QN]
        vals[rows, :] = kv[:, QN:]

    @pl.when(h == 0)
    def _():
        kcat[:, QN:QD] = rope_ref[...]
        stats[...] = jnp.zeros_like(stats)

    lane = lax.broadcasted_iota(jnp.int32, (QT, 128), 1)
    off = off_ref[...]
    for t in range(ROWS // QT):
        q = q_ref[0, pl.ds(t * QT, QT), :]
        top = jnp.full((QT, 128), NEG, jnp.float32)
        for i in range(KEYS // KT):
            rows = pl.ds(i * KT, KT)
            s = lax.dot_general(
                q, kcat[rows, 0:QD], (((1,), (1,)), ((), ())), preferred_element_type=jnp.float32
            )
            parts = []
            for b in range(QT // 64):
                thr = thr_ref[pl.ds(t * (QT // 64) + b, 1), rows]
                cols = []
                for c in range(KT // 128):
                    piece = s[b * 64 : (b + 1) * 64, c * 128 : (c + 1) * 128]
                    cols.append(jnp.where(off >= thr[:, c * 128 : (c + 1) * 128], piece, NEG))
                best = functools.reduce(jnp.maximum, cols)
                parts.append(best)
                for c in range(KT // 128):
                    sco[b * 64 : (b + 1) * 64, i * KT + c * 128 : i * KT + (c + 1) * 128] = cols[c]
            top = jnp.maximum(top, jnp.concatenate(parts, axis=0))
        m = jnp.max(top, axis=1, keepdims=True)
        mc = m * (SCALE * LOG2E)
        total = jnp.zeros((QT, 128), jnp.float32)
        acc = jnp.zeros((QT, VD), jnp.float32)
        for i in range(KEYS // KT):
            p = jnp.exp2(sco[:, pl.ds(i * KT, KT)] * (SCALE * LOG2E) - mc)
            for c in range(KT // 128):
                total = total + p[:, c * 128 : (c + 1) * 128]
            acc = acc + jnp.dot(
                p.astype(jnp.bfloat16),
                vals[pl.ds(i * KT, KT), :],
                preferred_element_type=jnp.float32,
            )
        den = jnp.sum(total, axis=1, keepdims=True)
        lse = m * SCALE + jnp.log(den)
        o_ref[pl.ds(t * QT, QT), pl.ds(pl.multiple_of(h * VD, VD), VD)] = (acc / den).astype(
            jnp.bfloat16
        )
        hi = lse.astype(jnp.bfloat16).astype(jnp.float32)
        mid = (lse - hi).astype(jnp.bfloat16).astype(jnp.float32)
        low = lse - hi - mid
        old = stats[pl.ds(t * QT, QT), :]
        old = jnp.where(lane == 3 * h, hi, old)
        old = jnp.where(lane == 3 * h + 1, mid, old)
        stats[pl.ds(t * QT, QT), :] = jnp.where(lane == 3 * h + 2, low, old)

    @pl.when(h == HEADS - 1)
    def _():
        o_ref[:, HEADS * VD :] = stats[...].astype(jnp.bfloat16)


def attend(q, lat, rope, weights, thr, off):
    full = lambda shape: pl.BlockSpec(shape, lambda h: tuple(0 for _ in shape))
    return pl.pallas_call(
        attend_kernel,
        grid=(HEADS,),
        out_shape=jax.ShapeDtypeStruct((ROWS, EXT), jnp.bfloat16),
        in_specs=[
            pl.BlockSpec((1, ROWS, QD), lambda h: (h, 0, 0)),
            full((KEYS, L)),
            full((KEYS, QR)),
            pl.BlockSpec((1, L, QN + VD), lambda h: (h, 0, 0)),
            full((CELLS, KEYS)),
            full((64, 128)),
        ],
        out_specs=full((ROWS, EXT)),
        scratch_shapes=[
            pltpu.VMEM((KEYS, QN + 128), jnp.bfloat16),
            pltpu.VMEM((KEYS, VD), jnp.bfloat16),
            pltpu.VMEM((QT, KEYS), jnp.float32),
            pltpu.VMEM((ROWS, 128), jnp.float32),
        ],
        compiler_params=pltpu.CompilerParams(vmem_limit_bytes=40 * 1024 * 1024),
        cost_estimate=pl.CostEstimate(
            flops=6_500_000_000, bytes_accessed=6_000_000, transcendentals=4_200_000
        ),
        name="attend",
    )(q, lat, rope, weights, thr, off)


def combine_kernel(x_ref, o_ref):
    n = GRP * TOK
    ext = [x_ref[pl.ds(c * n, n), pl.ds(HEADS * VD, 128)].astype(jnp.float32) for c in range(CELLS)]
    for h in range(HEADS):
        lse = [
            e[:, 3 * h : 3 * h + 1] + e[:, 3 * h + 1 : 3 * h + 2] + e[:, 3 * h + 2 : 3 * h + 3]
            for e in ext
        ]
        top = functools.reduce(jnp.maximum, lse)
        part = [jnp.exp(v - top) for v in lse]
        scale = 1.0 / functools.reduce(jnp.add, part)
        acc = jnp.zeros((n, VD), jnp.float32)
        for c in range(CELLS):
            acc = acc + x_ref[pl.ds(c * n, n), pl.ds(h * VD, VD)].astype(jnp.float32) * (
                part[c] * scale
            )
        o_ref[:, pl.ds(h * VD, VD)] = acc.astype(jnp.bfloat16)


def combine(x):
    return pl.pallas_call(
        combine_kernel,
        out_shape=jax.ShapeDtypeStruct((GRP * TOK, HEADS * VD), jnp.bfloat16),
        name="combine",
    )(x)


def shift(n, k):
    return [(i, (i + k) % n) for i in range(n)]


def gather_keys(piece):
    xn = [(a * 2 + b, (1 - a) * 2 + 1 - b) for a in range(2) for b in range(2)]
    other = lax.ppermute(piece, ("xl", "xh"), xn)
    own = jnp.stack([piece, other])
    up = down = own
    chunks = [own]
    for _ in range(3):
        up = lax.ppermute(up, "z", shift(ZN, 1))
        down = lax.ppermute(down, "z", shift(ZN, -1))
        chunks += [up, down]
    last = [lax.ppermute(up[0], "z", shift(ZN, 1)), lax.ppermute(down[1], "z", shift(ZN, -1))]
    chunks.append(jnp.stack(last))
    mine = jnp.stack(chunks)
    theirs = lax.ppermute(mine, "core", shift(CN, 1))
    return jnp.concatenate([mine, theirs]).reshape(KEYS, mine.shape[-1])


def thresholds(pattern, stripe):
    xl, y, core = lax.axis_index("xl"), lax.axis_index("y"), lax.axis_index("core")
    xh, z = lax.axis_index("xh"), lax.axis_index("z")
    ids = jnp.arange(SLOTS, dtype=jnp.int32)
    swap = ids % 2
    step = (ids // 2) % ZN
    k = core ^ (ids // (2 * ZN))
    back = jnp.where(step % 2 == 1, -((step + 1) // 2), step // 2)
    zz = (z + back) % ZN
    cell = ((xl ^ swap) * YN + y) * CN + k
    grp = (xh ^ swap) * ZN + zz
    place = cell * GRP + grp
    block = place * PER // BLOCK
    base = place * PER % BLOCK
    nb = stripe.shape[0]
    every = jnp.arange(nb, dtype=jnp.int32)
    kb = jnp.sum(jnp.where(block[:, None] == every[None, :], stripe[None, :], 0), axis=1)
    hit = jnp.sum(jnp.where(kb[None, :, None] == every[None, None, :], pattern[:, None, :], 0), axis=2)
    qb = nb - CELLS + jnp.arange(CELLS, dtype=jnp.int32)[:, None]
    see = (kb[None, :] < qb) & (hit == 1)
    offset = base[:, None] + jnp.arange(PER, dtype=jnp.int32)[None, :]
    thr = jnp.where(
        see[:, :, None], 0, jnp.where((kb[None, :] == qb)[:, :, None], offset[None], 4 * BLOCK)
    )
    return thr.reshape(CELLS, KEYS).astype(jnp.float32)


def body(queries, latents, key_rope, key_up, value_up, pattern, stripe):
    keys = gather_keys(jnp.concatenate([latents, key_rope], axis=1))
    send = queries.reshape(TOK, GRP, HEADS * QD).transpose(1, 0, 2)
    send = jnp.broadcast_to(send[None], (CELLS, GRP, TOK, HEADS * QD))
    send = send.reshape(CELLS * GRP, TOK, HEADS * QD)
    got = lax.all_to_all(send, CHIPS, split_axis=0, concat_axis=0, tiled=True)
    q = got.reshape(ROWS, HEADS, QD).transpose(1, 0, 2)
    weights = jnp.concatenate([key_up.transpose(0, 2, 1), value_up], axis=2)
    thr = thresholds(pattern, stripe)
    off = (lax.axis_index("core") * 64 + jnp.arange(64, dtype=jnp.int32)).astype(jnp.float32)
    off = jnp.broadcast_to(off[:, None], (64, 128))
    part = attend(q, keys[:, :L], keys[:, L:], weights, thr, off)
    back = lax.all_to_all(
        part.reshape(CELLS * GRP, TOK, EXT), CHIPS, split_axis=0, concat_axis=0, tiled=True
    )
    out = combine(back.reshape(CELLS * GRP * TOK, EXT))
    return out.reshape(GRP, TOK, HEADS * VD).transpose(1, 0, 2).reshape(TOK, GRP * HEADS * VD)


def solution(mesh):
    fine = Mesh(mesh.devices.reshape(XLN, YN, CN, XHN, ZN), AXES)
    in_specs = (
        P(AXES, None),
        P(AXES, None),
        P(AXES, None),
        P(("xh", "z"), None, None),
        P(("xh", "z"), None, None),
        P(),
        P(),
    )
    return jax.shard_map(body, mesh=fine, in_specs=in_specs, out_specs=P(AXES, None), check_vma=False)
```

```python
import functools
import math

import jax
import jax.numpy as jnp
from jax import lax
from jax.experimental import pallas as pl
from jax.experimental.pallas import tpu as pltpu
from jax.sharding import Mesh
from jax.sharding import PartitionSpec as P

L = 512
QN = 128
QR = 64
QD = QN + QR
VD = 128
BLOCK = 128
HEADS = 4
NEG = -1e30
SCALE = 1.0 / math.sqrt(QD)
LOG2E = math.log2(math.e)

AXES = ("xl", "y", "core", "xh", "z")
CHIPS = ("xl", "y", "xh", "z")
XLN, YN, CN, XHN, ZN = 2, 4, 2, 2, 8
CELLS = XLN * YN
GRP = XHN * ZN
PER = 64
TOK = 4
ROWS = CELLS * GRP * TOK
EXT = HEADS * VD + 128

QT = 256
KT = 512

FULL = 144
HALF = 80


def chunk(swap, other, step, full):
    return [(swap, other, step, j) for j in range(2 if full else 1)]


GROUP_A = [(0, 0, 0, True)]
GROUP_A += [(0, o, s, True) for s in (1, 2) for o in (0, 1)]
GROUP_A += [(1, o, 1, True) for o in (0, 1)]
GROUP_A += [(1, o, 0, False) for o in (0, 1)]
GROUP_B = [(x, o, 3, True) for x in (0, 1) for o in (0, 1)]
GROUP_B += [(1, o, 2, True) for o in (0, 1)]
GROUP_B += [(x, o, 4, False) for x in (0, 1) for o in (0, 1)]
PIECES = [p for c in GROUP_A + GROUP_B for p in chunk(*c)]
SLOTS = len(PIECES)
KEYS = SLOTS * PER
PART = KEYS // 2


def project_kernel(count, *refs):
    chunks, (w_ref, k_ref, v_ref, lat) = refs[:count], refs[count:]
    base = 0
    for ref in chunks:
        n = 2 * PER if ref.shape[0] == FULL else PER
        lat[base : base + n, :] = ref[0:n, :]
        for r in range(n // 16):
            rope = ref[n : n + 16, r * QR : (r + 1) * QR]
            for h in range(HEADS):
                k_ref[h, base + r * 16 : base + (r + 1) * 16, QN:QD] = rope
        base += n
    for h in range(HEADS):
        for i in range(PART // KT):
            rows = slice(i * KT, (i + 1) * KT)
            kv = jnp.dot(lat[rows, :], w_ref[h], preferred_element_type=jnp.float32)
            kv = kv.astype(jnp.bfloat16)
            k_ref[h, rows, 0:QN] = kv[:, 0:QN]
            v_ref[h, rows, :] = kv[:, QN:]


def project(chunks, weights):
    return pl.pallas_call(
        functools.partial(project_kernel, len(chunks)),
        out_shape=(
            jax.ShapeDtypeStruct((HEADS, PART, QD), jnp.bfloat16),
            jax.ShapeDtypeStruct((HEADS, PART, VD), jnp.bfloat16),
        ),
        scratch_shapes=[pltpu.VMEM((PART, L), jnp.bfloat16)],
        compiler_params=pltpu.CompilerParams(vmem_limit_bytes=24 * 1024 * 1024),
        cost_estimate=pl.CostEstimate(
            flops=1_100_000_000, bytes_accessed=5_000_000, transcendentals=0
        ),
        name="project",
    )(*chunks, weights)


def attend_kernel(q_ref, ka_ref, va_ref, kb_ref, vb_ref, thr_ref, off_ref, o_ref, qs, sco, stats):
    h = pl.program_id(0)

    @pl.when(h == 0)
    def _():
        for g in range(HEADS):
            qs[g] = q_ref[:, g * QD : (g + 1) * QD]
        stats[...] = jnp.zeros_like(stats)

    keys = [(r, slice(i * KT, (i + 1) * KT)) for r in (ka_ref, kb_ref) for i in range(PART // KT)]
    vals = [(r, slice(i * KT, (i + 1) * KT)) for r in (va_ref, vb_ref) for i in range(PART // KT)]
    lane = lax.broadcasted_iota(jnp.int32, (QT, 128), 1)
    off = off_ref[...]
    for t in range(ROWS // QT):
        q = qs[h, pl.ds(t * QT, QT), :]
        top = jnp.full((QT, 128), NEG, jnp.float32)
        for i, (ref, rows) in enumerate(keys):
            s = lax.dot_general(
                q, ref[0, rows, :], (((1,), (1,)), ((), ())), preferred_element_type=jnp.float32
            )
            parts = []
            for b in range(QT // 64):
                thr = thr_ref[pl.ds(t * (QT // 64) + b, 1), pl.ds(i * KT, KT)]
                cols = []
                for c in range(KT // 128):
                    piece = s[b * 64 : (b + 1) * 64, c * 128 : (c + 1) * 128]
                    cols.append(jnp.where(off >= thr[:, c * 128 : (c + 1) * 128], piece, NEG))
                best = functools.reduce(jnp.maximum, cols)
                parts.append(best)
                for c in range(KT // 128):
                    sco[b * 64 : (b + 1) * 64, i * KT + c * 128 : i * KT + (c + 1) * 128] = cols[c]
            top = jnp.maximum(top, jnp.concatenate(parts, axis=0))
        m = jnp.max(top, axis=1, keepdims=True)
        mc = m * (SCALE * LOG2E)
        total = jnp.zeros((QT, 128), jnp.float32)
        acc = jnp.zeros((QT, VD), jnp.float32)
        for i, (ref, rows) in enumerate(vals):
            p = jnp.exp2(sco[:, pl.ds(i * KT, KT)] * (SCALE * LOG2E) - mc)
            for c in range(KT // 128):
                total = total + p[:, c * 128 : (c + 1) * 128]
            acc = acc + jnp.dot(
                p.astype(jnp.bfloat16), ref[0, rows, :], preferred_element_type=jnp.float32
            )
        den = jnp.sum(total, axis=1, keepdims=True)
        lse = m * SCALE + jnp.log(den)
        o_ref[pl.ds(t * QT, QT), pl.ds(pl.multiple_of(h * VD, VD), VD)] = (acc / den).astype(
            jnp.bfloat16
        )
        hi = lse.astype(jnp.bfloat16).astype(jnp.float32)
        mid = (lse - hi).astype(jnp.bfloat16).astype(jnp.float32)
        low = lse - hi - mid
        old = stats[pl.ds(t * QT, QT), :]
        old = jnp.where(lane == 3 * h, hi, old)
        old = jnp.where(lane == 3 * h + 1, mid, old)
        stats[pl.ds(t * QT, QT), :] = jnp.where(lane == 3 * h + 2, low, old)

    @pl.when(h == HEADS - 1)
    def _():
        o_ref[:, HEADS * VD :] = stats[...].astype(jnp.bfloat16)


def attend(q, ka, va, kb, vb, thr, off):
    full = lambda shape: pl.BlockSpec(shape, lambda h: tuple(0 for _ in shape))
    head = lambda shape: pl.BlockSpec((1, *shape), lambda h: (h, 0, 0))
    return pl.pallas_call(
        attend_kernel,
        grid=(HEADS,),
        out_shape=jax.ShapeDtypeStruct((ROWS, EXT), jnp.bfloat16),
        in_specs=[
            full((ROWS, HEADS * QD)),
            head((PART, QD)),
            head((PART, VD)),
            head((PART, QD)),
            head((PART, VD)),
            full((CELLS, KEYS)),
            full((64, 128)),
        ],
        out_specs=full((ROWS, EXT)),
        scratch_shapes=[
            pltpu.VMEM((HEADS, ROWS, QD), jnp.bfloat16),
            pltpu.VMEM((QT, KEYS), jnp.float32),
            pltpu.VMEM((ROWS, 128), jnp.float32),
        ],
        compiler_params=pltpu.CompilerParams(vmem_limit_bytes=32 * 1024 * 1024),
        cost_estimate=pl.CostEstimate(
            flops=4_000_000_000, bytes_accessed=8_000_000, transcendentals=4_200_000
        ),
        name="attend",
    )(q, ka, va, kb, vb, thr, off)


def combine_kernel(x_ref, o_ref):
    n = GRP * TOK
    ext = [x_ref[pl.ds(c * n, n), pl.ds(HEADS * VD, 128)].astype(jnp.float32) for c in range(CELLS)]
    for h in range(HEADS):
        lse = [
            e[:, 3 * h : 3 * h + 1] + e[:, 3 * h + 1 : 3 * h + 2] + e[:, 3 * h + 2 : 3 * h + 3]
            for e in ext
        ]
        top = functools.reduce(jnp.maximum, lse)
        part = [jnp.exp(v - top) for v in lse]
        scale = 1.0 / functools.reduce(jnp.add, part)
        acc = jnp.zeros((n, VD), jnp.float32)
        for c in range(CELLS):
            acc = acc + x_ref[pl.ds(c * n, n), pl.ds(h * VD, VD)].astype(jnp.float32) * (
                part[c] * scale
            )
        o_ref[:, pl.ds(h * VD, VD)] = acc.astype(jnp.bfloat16)


def combine(x):
    return pl.pallas_call(
        combine_kernel,
        out_shape=jax.ShapeDtypeStruct((GRP * TOK, HEADS * VD), jnp.bfloat16),
        name="combine",
    )(x)


def shift(n, k):
    return [(i, (i + k) % n) for i in range(n)]


def gather_keys(latents, key_rope):
    near = [(a * 2 + b, (1 - a) * 2 + 1 - b) for a in range(2) for b in range(2)]
    round_z = [(i, (i + 1) % ZN) for i in range(ZN)] + [(ZN + i, ZN + (i - 1) % ZN) for i in range(ZN)]
    to_core = lambda x: lax.ppermute(x, "core", shift(CN, 1))
    to_near = lambda x: lax.ppermute(x, ("xl", "xh"), near)
    rope = key_rope.reshape(PER // 16, 16, QR).transpose(1, 0, 2).reshape(16, PER // 16 * QR)
    piece = jnp.concatenate([latents, jnp.pad(rope, ((0, 0), (0, L - rope.shape[1])))])
    mate = to_core(piece)
    got = {}
    got[1, 0, 0] = to_near(piece)
    side = jnp.concatenate([piece[PER:, : L // 2], mate[PER:, : L // 2]], axis=1)
    now = jnp.concatenate([piece[:PER], mate[:PER], side])
    got[0, 0, 0] = now
    for s in range(1, 5):
        if s == 4:
            now = jnp.concatenate([now[:PER], now[2 * PER :]])
        now = lax.ppermute(now, ("core", "z"), round_z)
        got[0, 0, s] = now
        got[1, 0, s] = to_near(now)
    for x in range(2):
        for s in range(5):
            if (x, s) != (0, 0):
                got[x, 1, s] = to_core(got[x, 0, s])
    pick = lambda group: [got[x, o, s] for x, o, s, _ in group]
    return pick(GROUP_A), pick(GROUP_B)


def thresholds(pattern, stripe):
    xl, y, core = lax.axis_index("xl"), lax.axis_index("y"), lax.axis_index("core")
    xh, z = lax.axis_index("xh"), lax.axis_index("z")
    swap, other, step, inner = (jnp.asarray([p[i] for p in PIECES], jnp.int32) for i in range(4))
    lane = core ^ other
    k = lane ^ inner
    zz = (z + jnp.where(lane == 1, step, ZN - step)) % ZN
    cell = ((xl ^ swap) * YN + y) * CN + k
    place = cell * GRP + (xh ^ swap) * ZN + zz
    block = place * PER // BLOCK
    base = place * PER % BLOCK
    nb = stripe.shape[0]
    every = jnp.arange(nb, dtype=jnp.int32)
    kb = jnp.sum(jnp.where(block[:, None] == every[None, :], stripe[None, :], 0), axis=1)
    hit = jnp.sum(jnp.where(kb[None, :, None] == every[None, None, :], pattern[:, None, :], 0), axis=2)
    qb = nb - CELLS + jnp.arange(CELLS, dtype=jnp.int32)[:, None]
    see = (kb[None, :] < qb) & (hit == 1)
    offset = base[:, None] + jnp.arange(PER, dtype=jnp.int32)[None, :]
    thr = jnp.where(
        see[:, :, None], 0, jnp.where((kb[None, :] == qb)[:, :, None], offset[None], 4 * BLOCK)
    )
    return thr.reshape(CELLS, KEYS).astype(jnp.float32)


def body(queries, latents, key_rope, key_up, value_up, pattern, stripe):
    cells = ("xl", "y")
    groups = ("xh", "z")
    send = queries.reshape(TOK, GRP, HEADS * QD).transpose(1, 0, 2)
    mine = lax.all_to_all(send, groups, split_axis=0, concat_axis=0, tiled=True)
    mine = mine.reshape(GRP * TOK, HEADS * QD)
    send = jnp.broadcast_to(mine[None], (CELLS, *mine.shape))
    q = lax.all_to_all(send, cells, split_axis=0, concat_axis=0, tiled=True)
    q = q.reshape(ROWS, HEADS * QD)
    weights = jnp.concatenate([key_up.transpose(0, 2, 1), value_up], axis=2)
    thr = thresholds(pattern, stripe)
    off = (lax.axis_index("core") * 64 + jnp.arange(64, dtype=jnp.int32)).astype(jnp.float32)
    off = jnp.broadcast_to(off[:, None], (64, 128))
    first, second = gather_keys(latents, key_rope)
    part = attend(q, *project(first, weights), *project(second, weights), thr, off)
    back = lax.all_to_all(
        part.reshape(CELLS, GRP * TOK, EXT), cells, split_axis=0, concat_axis=0, tiled=True
    )
    out = combine(back.reshape(ROWS, EXT)).reshape(GRP, TOK, HEADS * VD)
    out = lax.all_to_all(out, groups, split_axis=0, concat_axis=0, tiled=True)
    return out.transpose(1, 0, 2).reshape(TOK, GRP * HEADS * VD)


def solution(mesh):
    fine = Mesh(mesh.devices.reshape(XLN, YN, CN, XHN, ZN), AXES)
    in_specs = (
        P(AXES, None),
        P(AXES, None),
        P(AXES, None),
        P(("xh", "z"), None, None),
        P(("xh", "z"), None, None),
        P(),
        P(),
    )
    return jax.shard_map(body, mesh=fine, in_specs=in_specs, out_specs=P(AXES, None), check_vma=False)
```

```python
import functools
import math

import jax
import jax.numpy as jnp
from jax import lax
from jax.experimental import pallas as pl
from jax.experimental.pallas import tpu as pltpu
from jax.sharding import Mesh
from jax.sharding import PartitionSpec as P

L = 512
QN = 128
QR = 64
QD = QN + QR
VD = 128
BLOCK = 128
HEADS = 4
NEG = -1e30
SCALE = 1.0 / math.sqrt(QD)
LOG2E = math.log2(math.e)

AXES = ("xl", "y", "core", "xh", "z")
CHIPS = ("xl", "y", "xh", "z")
XLN, YN, CN, XHN, ZN = 2, 4, 2, 2, 8
CELLS = XLN * YN
GRP = XHN * ZN
PER = 64
TOK = 4
PEERS = CELLS * GRP
ROWS = PEERS * TOK
MSG = HEADS * VD
EXT = MSG + 128

VAT = 256
QT = 256
KT = 512

FULL = 144
HALF = 80


def chunk(swap, other, step, full):
    return [(swap, other, step, j) for j in range(2 if full else 1)]


GROUP_A = [(0, 0, 0, True)]
GROUP_A += [(0, o, s, True) for s in (1, 2) for o in (0, 1)]
GROUP_A += [(1, o, 1, True) for o in (0, 1)]
GROUP_A += [(1, o, 0, False) for o in (0, 1)]
GROUP_B = [(x, o, 3, True) for x in (0, 1) for o in (0, 1)]
GROUP_B += [(1, o, 2, True) for o in (0, 1)]
GROUP_B += [(x, o, 4, False) for x in (0, 1) for o in (0, 1)]
PIECES = [p for c in GROUP_A + GROUP_B for p in chunk(*c)]
SLOTS = len(PIECES)
KEYS = SLOTS * PER
PART = KEYS // 2


def unpack(chunks, lat, put_rope):
    base = 0
    for ref in chunks:
        n = 2 * PER if ref.shape[0] == FULL else PER
        lat[base : base + n, :] = ref[0:n, :]
        for r in range(n // 16):
            put_rope(base + r * 16, ref[n : n + 16, r * QR : (r + 1) * QR])
        base += n


def project_kernel(count, *refs):
    chunks, (w_ref, o_ref, lat) = refs[:count], refs[count:]

    def put_rope(row, rope):
        for h in range(HEADS):
            o_ref[h, row : row + 16, QN:QD] = rope

    unpack(chunks, lat, put_rope)
    for h in range(HEADS):
        for i in range(PART // KT):
            rows = slice(i * KT, (i + 1) * KT)
            kv = jnp.dot(lat[rows, :], w_ref[h], preferred_element_type=jnp.float32)
            kv = kv.astype(jnp.bfloat16)
            o_ref[h, rows, 0:QN] = kv[:, 0:QN]
            o_ref[h, rows, VAT:] = kv[:, QN:]


def project(chunks, weights):
    return pl.pallas_call(
        functools.partial(project_kernel, len(chunks)),
        out_shape=jax.ShapeDtypeStruct((HEADS, PART, VAT + VD), jnp.bfloat16),
        scratch_shapes=[pltpu.VMEM((PART, L), jnp.bfloat16)],
        compiler_params=pltpu.CompilerParams(vmem_limit_bytes=60 * 1024 * 1024),
        cost_estimate=pl.CostEstimate(
            flops=1_100_000_000, bytes_accessed=5_000_000, transcendentals=0
        ),
        name="project",
    )(*chunks, weights)


def attend_kernel(count, q_ref, ka_ref, *refs):
    chunks, refs = refs[:count], refs[count:]
    w_ref, thr_ref, o_ref, qs, ka, lat, side, kb, sco, stats, sems, more = refs
    h = pl.program_id(0)
    heads = [pltpu.make_async_copy(ka_ref.at[g], ka.at[g], sems.at[g]) for g in range(HEADS)]
    loads = []
    base = 0
    for j, ref in enumerate(chunks):
        n = 2 * PER if ref.shape[0] == FULL else PER
        loads.append(
            pltpu.make_async_copy(ref.at[0:n], lat.at[base : base + n], more.at[2 * j])
        )
        loads.append(pltpu.make_async_copy(ref.at[n : n + 16], side.at[j], more.at[2 * j + 1]))
        base += n

    @pl.when(h == 0)
    def _():
        for copy in [heads[0], *loads, *heads[1:]]:
            copy.start()
        for g in range(HEADS):
            qs[g] = q_ref[:, g * QD : (g + 1) * QD]
        stats[...] = jnp.zeros_like(stats)
        for copy in [heads[0], *loads]:
            copy.wait()
        row = 0
        for j, ref in enumerate(chunks):
            for r in range((2 * PER if ref.shape[0] == FULL else PER) // 16):
                kb[row : row + 16, QN:QD] = side[j, :, r * QR : (r + 1) * QR]
                row += 16

    for g in range(1, HEADS):

        @pl.when(h == g)
        def _():
            heads[g].wait()

    for i in range(PART // KT):
        rows = slice(i * KT, (i + 1) * KT)
        kv = jnp.dot(lat[rows, :], w_ref[0], preferred_element_type=jnp.float32)
        kv = kv.astype(jnp.bfloat16)
        kb[rows, 0:QN] = kv[:, 0:QN]
        kb[rows, VAT:] = kv[:, QN:]
    tiles = [(r, slice(i * KT, (i + 1) * KT)) for r in (ka.at[h], kb) for i in range(PART // KT)]
    lane = lax.broadcasted_iota(jnp.int32, (QT, 128), 1)
    off = lax.broadcasted_iota(jnp.int32, (64, 128), 0).astype(jnp.float32)
    for t in range(ROWS // QT):
        q = qs[h, pl.ds(t * QT, QT), :]
        top = jnp.full((QT, 128), NEG, jnp.float32)
        for i, (ref, rows) in enumerate(tiles):
            s = lax.dot_general(
                q, ref[rows, 0:QD], (((1,), (1,)), ((), ())), preferred_element_type=jnp.float32
            )
            parts = []
            for b in range(QT // 64):
                thr = thr_ref[pl.ds(t * (QT // 64) + b, 1), pl.ds(i * KT, KT)]
                cols = []
                for c in range(KT // 128):
                    piece = s[b * 64 : (b + 1) * 64, c * 128 : (c + 1) * 128]
                    cols.append(jnp.where(off >= thr[:, c * 128 : (c + 1) * 128], piece, NEG))
                parts.append(functools.reduce(jnp.maximum, cols))
                for c in range(KT // 128):
                    sco[t, b * 64 : (b + 1) * 64, i * KT + c * 128 : i * KT + (c + 1) * 128] = cols[c]
            top = jnp.maximum(top, jnp.concatenate(parts, axis=0))
        m = jnp.max(top, axis=1, keepdims=True)
        mc = m * (SCALE * LOG2E)
        total = jnp.zeros((QT, 128), jnp.float32)
        acc = jnp.zeros((QT, VD), jnp.float32)
        for i, (ref, rows) in enumerate(tiles):
            p = jnp.exp2(sco[t, :, pl.ds(i * KT, KT)] * (SCALE * LOG2E) - mc)
            for c in range(KT // 128):
                total = total + p[:, c * 128 : (c + 1) * 128]
            acc = acc + jnp.dot(
                p.astype(jnp.bfloat16), ref[rows, VAT:], preferred_element_type=jnp.float32
            )
        den = jnp.sum(total, axis=1, keepdims=True)
        lse = m * SCALE + jnp.log(den)
        o_ref[pl.ds(t * QT, QT), pl.ds(pl.multiple_of(h * VD, VD), VD)] = (acc / den).astype(
            jnp.bfloat16
        )
        hi = lse.astype(jnp.bfloat16).astype(jnp.float32)
        mid = (lse - hi).astype(jnp.bfloat16).astype(jnp.float32)
        low = lse - hi - mid
        old = stats[pl.ds(t * QT, QT), :]
        old = jnp.where(lane == 3 * h, hi, old)
        old = jnp.where(lane == 3 * h + 1, mid, old)
        stats[pl.ds(t * QT, QT), :] = jnp.where(lane == 3 * h + 2, low, old)

    @pl.when(h == HEADS - 1)
    def _():
        o_ref[:, MSG:] = stats[...].astype(jnp.bfloat16)


def attend(q, ka, chunks, weights, thr):
    full = lambda shape: pl.BlockSpec(shape, lambda h: tuple(0 for _ in shape))
    head = lambda shape: pl.BlockSpec((1, *shape), lambda h: (h, 0, 0))
    return pl.pallas_call(
        functools.partial(attend_kernel, len(chunks)),
        grid=(HEADS,),
        out_shape=jax.ShapeDtypeStruct((ROWS, EXT), jnp.bfloat16),
        in_specs=[
            full((ROWS, HEADS * QD)),
            pl.BlockSpec(memory_space=pltpu.HBM),
            *(pl.BlockSpec(memory_space=pltpu.HBM) for _ in chunks),
            head((L, QN + VD)),
            full((CELLS, KEYS)),
        ],
        out_specs=full((ROWS, EXT)),
        scratch_shapes=[
            pltpu.VMEM((HEADS, ROWS, QD), jnp.bfloat16),
            pltpu.VMEM((HEADS, PART, VAT + VD), jnp.bfloat16),
            pltpu.VMEM((PART, L), jnp.bfloat16),
            pltpu.VMEM((len(chunks), 16, L), jnp.bfloat16),
            pltpu.VMEM((PART, VAT + VD), jnp.bfloat16),
            pltpu.VMEM((ROWS // QT, QT, KEYS), jnp.float32),
            pltpu.VMEM((ROWS, 128), jnp.float32),
            pltpu.SemaphoreType.DMA((HEADS,)),
            pltpu.SemaphoreType.DMA((2 * len(chunks),)),
        ],
        compiler_params=pltpu.CompilerParams(vmem_limit_bytes=60 * 1024 * 1024),
        cost_estimate=pl.CostEstimate(
            flops=4_000_000_000, bytes_accessed=8_000_000, transcendentals=4_200_000
        ),
        name="attend",
    )(q, ka, *chunks, weights, thr)


def combine_kernel(x_ref, o_ref):
    n = GRP * TOK
    ext = [x_ref[pl.ds(c * n, n), MSG:].astype(jnp.float32) for c in range(CELLS)]
    for h in range(HEADS):
        j = 3 * h
        lse = [e[:, j : j + 1] + e[:, j + 1 : j + 2] + e[:, j + 2 : j + 3] for e in ext]
        top = functools.reduce(jnp.maximum, lse)
        part = [jnp.exp(v - top) for v in lse]
        scale = 1.0 / functools.reduce(jnp.add, part)
        acc = jnp.zeros((n, VD), jnp.float32)
        for c in range(CELLS):
            acc = acc + x_ref[pl.ds(c * n, n), pl.ds(h * VD, VD)].astype(jnp.float32) * (
                part[c] * scale
            )
        o_ref[:, :, pl.ds(h * VD, VD)] = acc.reshape(GRP, TOK, VD).astype(jnp.bfloat16)


def combine(x):
    return pl.pallas_call(
        combine_kernel,
        out_shape=jax.ShapeDtypeStruct((GRP, TOK, MSG), jnp.bfloat16),
        name="combine",
    )(x)


def pack_kernel(lat_ref, rope_ref, o_ref):
    o_ref[0:PER, :] = lat_ref[...]
    for r in range(L // QR):
        b = r % (PER // 16)
        o_ref[PER:HALF, r * QR : (r + 1) * QR] = rope_ref[b * 16 : (b + 1) * 16, :]


def pack(latents, key_rope):
    return pl.pallas_call(
        pack_kernel, out_shape=jax.ShapeDtypeStruct((HALF, L), jnp.bfloat16), name="pack"
    )(latents, key_rope)


def shift(n, k):
    return [(i, (i + k) % n) for i in range(n)]


def gather_keys(latents, key_rope):
    near = [(a * 2 + b, (1 - a) * 2 + 1 - b) for a in range(2) for b in range(2)]
    def round_z(x, n):
        up = [(i, (i + n) % ZN) for i in range(ZN)]
        down = [(ZN + i, ZN + (i - n) % ZN) for i in range(ZN)]
        return lax.ppermute(x, ("core", "z"), up + down)

    to_core = lambda x: lax.ppermute(x, "core", shift(CN, 1))
    to_near = lambda x: lax.ppermute(x, ("xl", "xh"), near)
    piece = pack(latents, key_rope)
    mate = to_core(piece)
    got = {}
    got[1, 0, 0] = to_near(piece)
    side = jnp.concatenate([piece[PER:, : L // 2], mate[PER:, : L // 2]], axis=1)
    now = jnp.concatenate([piece[:PER], mate[:PER], side])
    got[0, 0, 0] = now
    got[0, 0, 1] = round_z(now, 1)
    got[0, 0, 2] = now = round_z(now, 2)
    got[0, 0, 3] = round_z(now, 1)
    got[0, 0, 4] = round_z(jnp.concatenate([now[:PER], now[2 * PER :]]), 2)
    for s in range(1, 5):
        got[1, 0, s] = to_near(got[0, 0, s])
    for x in range(2):
        for s in range(5):
            if (x, s) != (0, 0):
                got[x, 1, s] = to_core(got[x, 0, s])
    pick = lambda group: [got[x, o, s] for x, o, s, _ in group]
    return pick(GROUP_A), pick(GROUP_B), now


def thresholds(pattern, stripe):
    xl, y, core = lax.axis_index("xl"), lax.axis_index("y"), lax.axis_index("core")
    xh, z = lax.axis_index("xh"), lax.axis_index("z")
    swap, other, step, inner = (jnp.asarray([p[i] for p in PIECES], jnp.int32) for i in range(4))
    lane = core ^ other
    k = lane ^ inner
    zz = (z + jnp.where(lane == 1, step, ZN - step)) % ZN
    cell = ((xl ^ swap) * YN + y) * CN + k
    place = cell * GRP + (xh ^ swap) * ZN + zz
    block = place * PER // BLOCK
    base = place * PER % BLOCK
    nb = stripe.shape[0]
    every = jnp.arange(nb, dtype=jnp.int32)
    kb = jnp.sum(jnp.where(block[:, None] == every[None, :], stripe[None, :], 0), axis=1)
    hit = jnp.sum(jnp.where(kb[None, :, None] == every[None, None, :], pattern[:, None, :], 0), axis=2)
    qb = nb - CELLS + jnp.arange(CELLS, dtype=jnp.int32)[:, None]
    see = (kb[None, :] < qb) & (hit == 1)
    offset = base[:, None] + jnp.arange(PER, dtype=jnp.int32)[None, :]
    thr = jnp.where(
        see[:, :, None], 0, jnp.where((kb[None, :] == qb)[:, :, None], offset[None], 4 * BLOCK)
    )
    return (thr - core * 64).reshape(CELLS, KEYS).astype(jnp.float32)


def body(queries, latents, key_rope, key_up, value_up, pattern, stripe):
    cells = ("xl", "y")
    groups = ("xh", "z")
    first, second, mark = gather_keys(latents, key_rope)
    send = queries.reshape(TOK, GRP, HEADS * QD).transpose(1, 0, 2)
    send, _ = lax.optimization_barrier((send, first[0]))
    mine = lax.all_to_all(send, groups, split_axis=0, concat_axis=0, tiled=True)
    mine = mine.reshape(GRP * TOK, HEADS * QD)
    send = jnp.broadcast_to(mine[None], (CELLS, *mine.shape))
    q = lax.all_to_all(send, cells, split_axis=0, concat_axis=0, tiled=True)
    q = q.reshape(ROWS, HEADS * QD)
    key_up, value_up, pattern, stripe, _ = lax.optimization_barrier(
        (key_up, value_up, pattern, stripe, mark)
    )
    weights = jnp.concatenate([key_up.transpose(0, 2, 1), value_up], axis=2)
    thr = thresholds(pattern, stripe)
    part = attend(q, project(first, weights), second, weights, thr)
    back = lax.all_to_all(
        part.reshape(CELLS, GRP * TOK, EXT), cells, split_axis=0, concat_axis=0, tiled=True
    )
    out = lax.all_to_all(combine(back.reshape(ROWS, EXT)), groups, split_axis=0, concat_axis=0, tiled=True)
    return out.transpose(1, 0, 2).reshape(TOK, GRP * MSG)


def solution(mesh):
    fine = Mesh(mesh.devices.reshape(XLN, YN, CN, XHN, ZN), AXES)
    in_specs = (
        P(AXES, None),
        P(AXES, None),
        P(AXES, None),
        P(("xh", "z"), None, None),
        P(("xh", "z"), None, None),
        P(),
        P(),
    )
    return jax.shard_map(body, mesh=fine, in_specs=in_specs, out_specs=P(AXES, None), check_vma=False)
```

```python
import functools
import math

import jax
import jax.numpy as jnp
from jax import lax
from jax.experimental import pallas as pl
from jax.experimental.pallas import tpu as pltpu
from jax.sharding import Mesh
from jax.sharding import PartitionSpec as P

L = 512
QN = 128
QR = 64
QD = QN + QR
VD = 128
BLOCK = 128
HEADS = 4
NEG = -1e30
SCALE = 1.0 / math.sqrt(QD)
LOG2E = math.log2(math.e)

AXES = ("xl", "y", "core", "xh", "z")
XLN, YN, CN, XHN, ZN = 2, 4, 2, 2, 8
CELLS = XLN * YN
GRP = XHN * ZN
PER = 64
TOK = 4
ROWS = CELLS * GRP * TOK
MSG = HEADS * VD
EXT = MSG + 128

HALF = 80
FOUR = 4 * PER
FULL = FOUR + 32

CHUNKS = [(0, 0)] + [(o, s) for s in (1, 2, 3) for o in (0, 1)] + [(0, 4)]
PIECES = [(j % 2, o, s, j // 2) for o, s in CHUNKS for j in range(4)]
SLOTS = len(PIECES)
KEYS = SLOTS * PER

VAT = 256
QT = 256
KT = 512


def attend_kernel(q_ref, *refs):
    chunks, refs = refs[: len(CHUNKS)], refs[len(CHUNKS) :]
    w_ref, thr_ref, o_ref, kv, sco = refs
    units = [(h, t) for h in range(HEADS) for t in range(ROWS // QT)]
    tiles = KEYS // KT
    off = lax.broadcasted_iota(jnp.int32, (64, 128), 0).astype(jnp.float32)
    lane = lax.broadcasted_iota(jnp.int32, (QT, 128), 1)

    def project(h, c):
        new = jnp.dot(chunks[c][0:FOUR, :], w_ref[h], preferred_element_type=jnp.float32)
        new = new.astype(jnp.bfloat16)
        rows = slice(c * FOUR, (c + 1) * FOUR)
        kv[h % 2, rows, 0:QN] = new[:, 0:QN]
        kv[h % 2, rows, VAT:] = new[:, QN:]

    for c in range(len(CHUNKS)):
        for r in range(FOUR // 16):
            at = FOUR + 16 * (r // 8)
            rope = chunks[c][at : at + 16, (r % 8) * QR : (r % 8 + 1) * QR]
            for b in range(2):
                kv[b, c * FOUR + r * 16 : c * FOUR + (r + 1) * 16, QN:QD] = rope
        project(0, c)

    def score(u, i, top):
        h, t = units[u]
        q = q_ref[t * QT : (t + 1) * QT, h * QD : (h + 1) * QD]
        s = lax.dot_general(
            q,
            kv[h % 2, i * KT : (i + 1) * KT, 0:QD],
            (((1,), (1,)), ((), ())),
            preferred_element_type=jnp.float32,
        )
        parts = []
        for b in range(QT // 64):
            row = t * (QT // 64) + b
            thr = thr_ref[row : row + 1, i * KT : (i + 1) * KT]
            cols = []
            for c in range(KT // 128):
                piece = s[b * 64 : (b + 1) * 64, c * 128 : (c + 1) * 128]
                cols.append(jnp.where(off >= thr[:, c * 128 : (c + 1) * 128], piece, NEG))
            parts.append(functools.reduce(jnp.maximum, cols))
            for c in range(KT // 128):
                at = i * KT + c * 128
                sco[u % 2, b * 64 : (b + 1) * 64, at : at + 128] = cols[c]
        best = jnp.concatenate(parts, axis=0)
        return best if top is None else jnp.maximum(top, best)

    def mix(u, i, mc, total, acc):
        h, t = units[u]
        p = jnp.exp2(sco[u % 2, :, i * KT : (i + 1) * KT] * (SCALE * LOG2E) - mc)
        for c in range(KT // 128):
            piece = p[:, c * 128 : (c + 1) * 128]
            total = piece if total is None else total + piece
        new = jnp.dot(
            p.astype(jnp.bfloat16),
            kv[h % 2, i * KT : (i + 1) * KT, VAT:],
            preferred_element_type=jnp.float32,
        )
        return total, new if acc is None else acc + new

    stats = [jnp.zeros((QT, 128), jnp.float32) for _ in range(ROWS // QT)]
    m = None
    for u in range(len(units) + 1):
        top = total = acc = None
        if u:
            mc = m * (SCALE * LOG2E)
        for i in range(tiles):
            if u < len(units):
                top = score(u, i, top)
            if u:
                total, acc = mix(u - 1, i, mc, total, acc)
            if u < len(units):
                h, t = units[u]
                if t == ROWS // QT - 1 and h + 1 < HEADS:
                    each = len(CHUNKS) // tiles
                    for c in range(i * each, (i + 1) * each):
                        project(h + 1, c)
        if u:
            h, t = units[u - 1]
            den = jnp.sum(total, axis=1, keepdims=True)
            lse = m * SCALE + jnp.log(den)
            o_ref[t * QT : (t + 1) * QT, h * VD : (h + 1) * VD] = (acc / den).astype(jnp.bfloat16)
            hi = lse.astype(jnp.bfloat16).astype(jnp.float32)
            mid = (lse - hi).astype(jnp.bfloat16).astype(jnp.float32)
            old = jnp.where(lane == 3 * h, hi, stats[t])
            old = jnp.where(lane == 3 * h + 1, mid, old)
            stats[t] = jnp.where(lane == 3 * h + 2, lse - hi - mid, old)
        if u < len(units):
            m = jnp.max(top, axis=1, keepdims=True)
    for t in range(ROWS // QT):
        o_ref[t * QT : (t + 1) * QT, MSG:] = stats[t].astype(jnp.bfloat16)


def attend(q, chunks, weights, thr):
    return pl.pallas_call(
        attend_kernel,
        out_shape=jax.ShapeDtypeStruct((ROWS, EXT), jnp.bfloat16),
        scratch_shapes=[
            pltpu.VMEM((2, KEYS, VAT + VD), jnp.bfloat16),
            pltpu.VMEM((2, QT, KEYS), jnp.float32),
        ],
        compiler_params=pltpu.CompilerParams(vmem_limit_bytes=32 * 1024 * 1024),
        cost_estimate=pl.CostEstimate(
            flops=6_500_000_000, bytes_accessed=6_000_000, transcendentals=4_200_000
        ),
        name="attend",
    )(q, *chunks, weights, thr)


def combine_kernel(x_ref, o_ref):
    n = GRP * TOK
    ext = [x_ref[pl.ds(c * n, n), MSG:].astype(jnp.float32) for c in range(CELLS)]
    for h in range(HEADS):
        j = 3 * h
        lse = [e[:, j : j + 1] + e[:, j + 1 : j + 2] + e[:, j + 2 : j + 3] for e in ext]
        top = functools.reduce(jnp.maximum, lse)
        part = [jnp.exp(v - top) for v in lse]
        scale = 1.0 / functools.reduce(jnp.add, part)
        acc = jnp.zeros((n, VD), jnp.float32)
        for c in range(CELLS):
            acc = acc + x_ref[pl.ds(c * n, n), pl.ds(h * VD, VD)].astype(jnp.float32) * (
                part[c] * scale
            )
        o_ref[:, :, pl.ds(h * VD, VD)] = acc.reshape(GRP, TOK, VD).astype(jnp.bfloat16)


def combine(x):
    return pl.pallas_call(
        combine_kernel,
        out_shape=jax.ShapeDtypeStruct((GRP, TOK, MSG), jnp.bfloat16),
        name="combine",
    )(x)


def pack_kernel(lat_ref, rope_ref, o_ref):
    o_ref[0:PER, :] = lat_ref[...]
    for r in range(L // QR):
        b = r % (PER // 16)
        o_ref[PER:HALF, r * QR : (r + 1) * QR] = rope_ref[b * 16 : (b + 1) * 16, :]


def pack(latents, key_rope):
    return pl.pallas_call(
        pack_kernel, out_shape=jax.ShapeDtypeStruct((HALF, L), jnp.bfloat16), name="pack"
    )(latents, key_rope)


def merge_kernel(*refs):
    o_ref = refs[-1]
    for j, ref in enumerate(refs[:-1]):
        half = slice(j % 2 * (L // 2), (j % 2 + 1) * (L // 2))
        at = FOUR + j // 2 * 16
        o_ref[j * PER : (j + 1) * PER, :] = ref[0:PER, :]
        o_ref[at : at + 16, half] = ref[PER:HALF, half]


def merge(pieces):
    return pl.pallas_call(
        merge_kernel, out_shape=jax.ShapeDtypeStruct((FULL, L), jnp.bfloat16), name="merge"
    )(*pieces)


def shift(n, k):
    return [(i, (i + k) % n) for i in range(n)]


def gather_keys(latents, key_rope, swap):
    near = [(a * 2 + b, (1 - a) * 2 + 1 - b) for a in range(2) for b in range(2)]
    up = [(i, (i + 1) % ZN) for i in range(ZN)]
    down = [(ZN + i, ZN + (i - 1) % ZN) for i in range(ZN)]
    to_core = lambda x: lax.ppermute(x, "core", shift(CN, 1))
    piece = pack(latents, key_rope)
    beside = lax.ppermute(piece, ("xl", "xh"), near)
    pieces = [piece, beside, to_core(piece), to_core(beside)]
    mine = swap(piece)
    pieces, mine = lax.optimization_barrier((pieces, mine))
    now = merge(pieces)
    got = {(0, 0): now}
    for s in range(1, 5):
        got[0, s] = now = lax.ppermute(now, ("core", "z"), up + down)
        if s < 4:
            got[1, s] = to_core(now)
    return [got[c] for c in CHUNKS], mine, got[0, 1]


def threshold_kernel(pattern_ref, stripe_ref, o_ref):
    xl, y, core = lax.axis_index("xl"), lax.axis_index("y"), lax.axis_index("core")
    xh, z = lax.axis_index("xh"), lax.axis_index("z")
    lane = lax.broadcasted_iota(jnp.int32, (1, 128), 1)
    blocks = stripe_ref.shape[0]

    def facts(swap, other, step, inner):
        side = core ^ other
        zz = lax.rem(z + jnp.where(side == 1, step, ZN - step), ZN)
        cell = ((xl ^ swap) * YN + y) * CN + (side ^ inner)
        place = cell * GRP + (xh ^ swap) * ZN + zz
        return stripe_ref[lax.shift_right_logical(place, 1)], (place & 1) * PER - core * 64

    for pair in range(SLOTS // 2):
        two = [facts(*PIECES[2 * pair + j]) for j in range(2)]
        for r in range(CELLS):
            vals = []
            for j, (kb, base) in enumerate(two):
                see = (kb < blocks - CELLS + r) & (pattern_ref[r, kb] == 1)
                same = kb == blocks - CELLS + r
                const = jnp.where(see, -BLOCK, jnp.where(same, base - j * PER, 4 * BLOCK))
                vals.append(const + lane * jnp.where(same, 1, 0))
            row = jnp.where(lane < PER, vals[0], vals[1]).astype(jnp.float32)
            o_ref[r : r + 1, pair * 128 : (pair + 1) * 128] = row


def thresholds(pattern, stripe):
    return pl.pallas_call(
        threshold_kernel,
        out_shape=jax.ShapeDtypeStruct((CELLS, KEYS), jnp.float32),
        in_specs=[pl.BlockSpec(memory_space=pltpu.SMEM)] * 2,
        name="thresholds",
    )(pattern, stripe)


def body(queries, latents, key_rope, key_up, value_up, pattern, stripe):
    cells = ("xl", "y")
    groups = ("xh", "z")
    def swap(after):
        send = queries.reshape(TOK, GRP, HEADS * QD).transpose(1, 0, 2)
        send, _ = lax.optimization_barrier((send, after))
        return lax.all_to_all(send, groups, split_axis=0, concat_axis=0, tiled=True)

    chunks, mine, mark = gather_keys(latents, key_rope, swap)
    mine = mine.reshape(GRP * TOK, HEADS * QD)
    send = jnp.broadcast_to(mine[None], (CELLS, *mine.shape))
    q = lax.all_to_all(send, cells, split_axis=0, concat_axis=0, tiled=True)
    q = q.reshape(ROWS, HEADS * QD)
    key_up, value_up, pattern, stripe, _ = lax.optimization_barrier(
        (key_up, value_up, pattern, stripe, mark)
    )
    weights = jnp.concatenate([key_up.transpose(0, 2, 1), value_up], axis=2)
    part = attend(q, chunks, weights, thresholds(pattern, stripe))
    back = lax.all_to_all(
        part.reshape(CELLS, GRP * TOK, EXT), cells, split_axis=0, concat_axis=0, tiled=True
    )
    out = lax.all_to_all(combine(back.reshape(ROWS, EXT)), groups, split_axis=0, concat_axis=0, tiled=True)
    return out.transpose(1, 0, 2).reshape(TOK, GRP * MSG)


def solution(mesh):
    fine = Mesh(mesh.devices.reshape(XLN, YN, CN, XHN, ZN), AXES)
    in_specs = (
        P(AXES, None),
        P(AXES, None),
        P(AXES, None),
        P(("xh", "z"), None, None),
        P(("xh", "z"), None, None),
        P(),
        P(),
    )
    return jax.shard_map(body, mesh=fine, in_specs=in_specs, out_specs=P(AXES, None), check_vma=False)
```

```python
import functools
import math

import jax
import jax.numpy as jnp
from jax import lax
from jax.experimental import pallas as pl
from jax.experimental.pallas import tpu as pltpu
from jax.sharding import Mesh
from jax.sharding import PartitionSpec as P

L = 512
QN = 128
QR = 64
QD = QN + QR
VD = 128
BLOCK = 128
HEADS = 4
NEG = -1e30
SCALE = 1.0 / math.sqrt(QD)
LOG2E = math.log2(math.e)

AXES = ("xl", "y", "core", "xh", "z")
XLN, YN, CN, XHN, ZN = 2, 4, 2, 2, 8
CELLS = XLN * YN
GRP = XHN * ZN
PER = 64
TOK = 4
ROWS = CELLS * GRP * TOK
MSG = HEADS * VD
EXT = MSG + 128

HALF = 80
FOUR = 4 * PER
FULL = FOUR + 32

EARLY = [(0, 0)] + [(o, s) for s in (1, 2) for o in (0, 1)]
LATE = [(0, 3), (1, 3), (0, 4)]
CHUNKS = EARLY + LATE
PIECES = [(j % 2, o, s, j // 2) for o, s in CHUNKS for j in range(4)]
SLOTS = len(PIECES)
KEYS = SLOTS * PER

VAT = 256
QT = 256
KT = FOUR
SMALL = pltpu.CompilerParams(vmem_limit_bytes=8 * 1024 * 1024)


def attend_kernel(count, first, *refs):
    chunks, refs = refs[:count], refs[count:]
    if first:
        q_ref, w_ref, thr_ref, old_ref, lse_ref, o_ref, kv, sco = refs
    else:
        q_ref, w_ref, thr_ref, o_ref, lse_ref, kv, sco = refs
    units = [(h, t) for h in range(HEADS) for t in range(ROWS // QT)]
    off = lax.broadcasted_iota(jnp.int32, (64, 128), 0).astype(jnp.float32)
    lane = lax.broadcasted_iota(jnp.int32, (QT, 128), 1)

    def project(h, c):
        new = jnp.dot(chunks[c][0:FOUR, :], w_ref[h], preferred_element_type=jnp.float32)
        new = new.astype(jnp.bfloat16)
        rows = slice(c * FOUR, (c + 1) * FOUR)
        kv[h % 2, rows, 0:QN] = new[:, 0:QN]
        kv[h % 2, rows, VAT:] = new[:, QN:]

    for c in range(count):
        for r in range(FOUR // 16):
            at = FOUR + 16 * (r // 8)
            rope = chunks[c][at : at + 16, (r % 8) * QR : (r % 8 + 1) * QR]
            for b in range(2):
                kv[b, c * FOUR + r * 16 : c * FOUR + (r + 1) * 16, QN:QD] = rope
        project(0, c)

    def score(u, i, top):
        h, t = units[u]
        q = q_ref[t * QT : (t + 1) * QT, h * QD : (h + 1) * QD]
        s = lax.dot_general(
            q,
            kv[h % 2, i * KT : (i + 1) * KT, 0:QD],
            (((1,), (1,)), ((), ())),
            preferred_element_type=jnp.float32,
        )
        parts = []
        for b in range(QT // 64):
            row = t * (QT // 64) + b
            at = (first + i) * KT
            thr = thr_ref[row : row + 1, at : at + KT]
            cols = []
            for c in range(KT // 128):
                piece = s[b * 64 : (b + 1) * 64, c * 128 : (c + 1) * 128]
                cols.append(jnp.where(off >= thr[:, c * 128 : (c + 1) * 128], piece, NEG))
            parts.append(functools.reduce(jnp.maximum, cols))
            for c in range(KT // 128):
                at = i * KT + c * 128
                sco[u % 2, b * 64 : (b + 1) * 64, at : at + 128] = cols[c]
        best = jnp.concatenate(parts, axis=0)
        return best if top is None else jnp.maximum(top, best)

    def mix(u, i, mc, total, acc):
        h, t = units[u]
        p = jnp.exp2(sco[u % 2, :, i * KT : (i + 1) * KT] * (SCALE * LOG2E) - mc)
        for c in range(KT // 128):
            piece = p[:, c * 128 : (c + 1) * 128]
            total = piece if total is None else total + piece
        new = jnp.dot(
            p.astype(jnp.bfloat16),
            kv[h % 2, i * KT : (i + 1) * KT, VAT:],
            preferred_element_type=jnp.float32,
        )
        return total, new if acc is None else acc + new

    stats = [jnp.zeros((QT, 128), jnp.float32) for _ in range(ROWS // QT)]
    m = None
    for u in range(len(units) + 1):
        top = total = acc = None
        if u:
            mc = m * (SCALE * LOG2E)
        for i in range(count):
            if u < len(units):
                top = score(u, i, top)
            if u:
                total, acc = mix(u - 1, i, mc, total, acc)
            if u < len(units):
                h, t = units[u]
                if t == ROWS // QT - 1 and h + 1 < HEADS:
                    project(h + 1, i)
        if u:
            h, t = units[u - 1]
            rows = slice(t * QT, (t + 1) * QT)
            den = jnp.sum(total, axis=1, keepdims=True)
            lse = m * SCALE + jnp.log(den)
            out = acc / den
            cols = slice(h * VD, (h + 1) * VD)
            if first:
                before = lse_ref[rows, h : h + 1]
                both = jnp.maximum(before, lse)
                part, rest = jnp.exp(lse - both), jnp.exp(before - both)
                out = (out * part + old_ref[rows, cols] * rest) / (part + rest)
                lse = both + jnp.log(part + rest)
                hi = lse.astype(jnp.bfloat16).astype(jnp.float32)
                mid = (lse - hi).astype(jnp.bfloat16).astype(jnp.float32)
                old = jnp.where(lane == 3 * h, hi, stats[t])
                old = jnp.where(lane == 3 * h + 1, mid, old)
                stats[t] = jnp.where(lane == 3 * h + 2, lse - hi - mid, old)
            else:
                stats[t] = jnp.where(lane == h, lse, stats[t])
            o_ref[rows, cols] = out.astype(o_ref.dtype)
        if u < len(units):
            m = jnp.max(top, axis=1, keepdims=True)
    for t in range(ROWS // QT):
        if first:
            o_ref[t * QT : (t + 1) * QT, MSG:] = stats[t].astype(jnp.bfloat16)
        else:
            lse_ref[t * QT : (t + 1) * QT, :] = stats[t]


def attend(chunks, q, weights, thr, before=()):
    count = len(chunks)
    first = len(CHUNKS) - count if before else 0
    if before:
        shape = jax.ShapeDtypeStruct((ROWS, EXT), jnp.bfloat16)
    else:
        shape = (
            jax.ShapeDtypeStruct((ROWS, MSG), jnp.float32),
            jax.ShapeDtypeStruct((ROWS, 128), jnp.float32),
        )
    return pl.pallas_call(
        functools.partial(attend_kernel, count, first),
        out_shape=shape,
        scratch_shapes=[
            pltpu.VMEM((2, count * FOUR, VAT + VD), jnp.bfloat16),
            pltpu.VMEM((2, QT, count * FOUR), jnp.float32),
        ],
        compiler_params=pltpu.CompilerParams(vmem_limit_bytes=24 * 1024 * 1024),
        cost_estimate=pl.CostEstimate(
            flops=1_000_000 * count, bytes_accessed=1_000 * count, transcendentals=1_000 * count
        ),
        name="attend_late" if before else "attend_early",
    )(*chunks, q, weights, thr, *before)


def combine_kernel(x_ref, o_ref):
    n = GRP * TOK
    ext = [x_ref[pl.ds(c * n, n), MSG:].astype(jnp.float32) for c in range(CELLS)]
    for h in range(HEADS):
        j = 3 * h
        lse = [e[:, j : j + 1] + e[:, j + 1 : j + 2] + e[:, j + 2 : j + 3] for e in ext]
        top = functools.reduce(jnp.maximum, lse)
        part = [jnp.exp(v - top) for v in lse]
        scale = 1.0 / functools.reduce(jnp.add, part)
        acc = jnp.zeros((n, VD), jnp.float32)
        for c in range(CELLS):
            acc = acc + x_ref[pl.ds(c * n, n), pl.ds(h * VD, VD)].astype(jnp.float32) * (
                part[c] * scale
            )
        o_ref[:, :, pl.ds(h * VD, VD)] = acc.reshape(GRP, TOK, VD).astype(jnp.bfloat16)


def combine(x):
    return pl.pallas_call(
        combine_kernel,
        out_shape=jax.ShapeDtypeStruct((GRP, TOK, MSG), jnp.bfloat16),
        compiler_params=SMALL,
        name="combine",
    )(x)


def pack_kernel(lat_ref, rope_ref, o_ref):
    o_ref[0:PER, :] = lat_ref[...]
    for r in range(L // QR):
        b = r % (PER // 16)
        o_ref[PER:HALF, r * QR : (r + 1) * QR] = rope_ref[b * 16 : (b + 1) * 16, :]


def pack(latents, key_rope):
    return pl.pallas_call(
        pack_kernel,
        out_shape=jax.ShapeDtypeStruct((HALF, L), jnp.bfloat16),
        compiler_params=SMALL,
        name="pack",
    )(latents, key_rope)


def merge_kernel(*refs):
    o_ref = refs[-1]
    for j, ref in enumerate(refs[:-1]):
        half = slice(j % 2 * (L // 2), (j % 2 + 1) * (L // 2))
        at = FOUR + j // 2 * 16
        o_ref[j * PER : (j + 1) * PER, :] = ref[0:PER, :]
        o_ref[at : at + 16, half] = ref[PER:HALF, half]


def merge(pieces):
    return pl.pallas_call(
        merge_kernel,
        out_shape=jax.ShapeDtypeStruct((FULL, L), jnp.bfloat16),
        compiler_params=SMALL,
        name="merge",
    )(*pieces)


def shift(n, k):
    return [(i, (i + k) % n) for i in range(n)]


def gather_keys(latents, key_rope, swap):
    near = [(a * 2 + b, (1 - a) * 2 + 1 - b) for a in range(2) for b in range(2)]
    to_core = lambda x: lax.ppermute(x, "core", shift(CN, 1))

    def round_z(x, n):
        up = [(i, (i + n) % ZN) for i in range(ZN)]
        down = [(ZN + i, ZN + (i - n) % ZN) for i in range(ZN)]
        return lax.ppermute(x, ("core", "z"), up + down)

    piece = pack(latents, key_rope)
    beside, mate = lax.ppermute(piece, ("xl", "xh"), near), to_core(piece)
    pieces = [piece, beside, mate, to_core(beside)]
    mine = swap(mate)
    pieces, mine = lax.optimization_barrier((pieces, mine))
    now = merge(pieces)
    got = {(0, 0): now, (0, 1): round_z(now, 1), (0, 2): round_z(now, 2)}
    got[0, 3] = round_z(got[0, 2], 1)
    got[0, 4] = round_z(got[0, 2], 2)
    for s in (1, 2):
        got[1, s] = to_core(got[0, s])
    return got, to_core, mine, beside


def threshold_kernel(pattern_ref, stripe_ref, o_ref):
    xl, y, core = lax.axis_index("xl"), lax.axis_index("y"), lax.axis_index("core")
    xh, z = lax.axis_index("xh"), lax.axis_index("z")
    lane = lax.broadcasted_iota(jnp.int32, (1, 128), 1)
    blocks = stripe_ref.shape[0]

    def facts(swap, other, step, inner):
        side = core ^ other
        zz = lax.rem(z + jnp.where(side == 1, step, ZN - step), ZN)
        cell = ((xl ^ swap) * YN + y) * CN + (side ^ inner)
        place = cell * GRP + (xh ^ swap) * ZN + zz
        return stripe_ref[lax.shift_right_logical(place, 1)], (place & 1) * PER - core * 64

    for pair in range(SLOTS // 2):
        two = [facts(*PIECES[2 * pair + j]) for j in range(2)]
        for r in range(CELLS):
            vals = []
            for j, (kb, base) in enumerate(two):
                see = (kb < blocks - CELLS + r) & (pattern_ref[r, kb] == 1)
                same = kb == blocks - CELLS + r
                const = jnp.where(see, -BLOCK, jnp.where(same, base - j * PER, 4 * BLOCK))
                vals.append(const + lane * jnp.where(same, 1, 0))
            row = jnp.where(lane < PER, vals[0], vals[1]).astype(jnp.float32)
            o_ref[r : r + 1, pair * 128 : (pair + 1) * 128] = row


def thresholds(pattern, stripe):
    return pl.pallas_call(
        threshold_kernel,
        out_shape=jax.ShapeDtypeStruct((CELLS, KEYS), jnp.float32),
        in_specs=[pl.BlockSpec(memory_space=pltpu.SMEM)] * 2,
        compiler_params=SMALL,
        name="thresholds",
    )(pattern, stripe)


def body(queries, latents, key_rope, key_up, value_up, pattern, stripe):
    cells = ("xl", "y")
    groups = ("xh", "z")
    def swap(after):
        send = queries.reshape(TOK, GRP, HEADS * QD).transpose(1, 0, 2)
        send, _ = lax.optimization_barrier((send, after))
        return lax.all_to_all(send, groups, split_axis=0, concat_axis=0, tiled=True)

    got, to_core, mine, mark = gather_keys(latents, key_rope, swap)
    mine = mine.reshape(GRP * TOK, HEADS * QD)
    send = jnp.broadcast_to(mine[None], (CELLS, *mine.shape))
    q = lax.all_to_all(send, cells, split_axis=0, concat_axis=0, tiled=True)
    q = q.reshape(ROWS, HEADS * QD)
    key_up, value_up, pattern, stripe, _ = lax.optimization_barrier(
        (key_up, value_up, pattern, stripe, mark)
    )
    weights = jnp.concatenate([key_up.transpose(0, 2, 1), value_up], axis=2)
    thr = thresholds(pattern, stripe)
    before = attend([got[c] for c in EARLY], q, weights, thr)
    (got[0, 3], got[0, 4]), before = lax.optimization_barrier(((got[0, 3], got[0, 4]), before))
    got[1, 3] = to_core(got[0, 3])
    part = attend([got[c] for c in LATE], q, weights, thr, before)
    back = lax.all_to_all(
        part.reshape(CELLS, GRP * TOK, EXT), cells, split_axis=0, concat_axis=0, tiled=True
    )
    out = lax.all_to_all(combine(back.reshape(ROWS, EXT)), groups, split_axis=0, concat_axis=0, tiled=True)
    return out.transpose(1, 0, 2).reshape(TOK, GRP * MSG)


def solution(mesh):
    fine = Mesh(mesh.devices.reshape(XLN, YN, CN, XHN, ZN), AXES)
    in_specs = (
        P(AXES, None),
        P(AXES, None),
        P(AXES, None),
        P(("xh", "z"), None, None),
        P(("xh", "z"), None, None),
        P(),
        P(),
    )
    return jax.shard_map(body, mesh=fine, in_specs=in_specs, out_specs=P(AXES, None), check_vma=False)
```

```python
import functools
import math

import jax
import jax.numpy as jnp
from jax import lax
from jax.experimental import pallas as pl
from jax.experimental.pallas import tpu as pltpu
from jax.sharding import Mesh
from jax.sharding import PartitionSpec as P

L = 512
QN = 128
QR = 64
QD = QN + QR
VD = 128
BLOCK = 128
HEADS = 4
NEG = -1e30
SCALE = 1.0 / math.sqrt(QD)
LOG2E = math.log2(math.e)

AXES = ("xl", "y", "core", "xh", "z")
XLN, YN, CN, XHN, ZN = 2, 4, 2, 2, 8
CELLS = XLN * YN
GRP = XHN * ZN
PER = 64
TOK = 4
ROWS = CELLS * GRP * TOK
MSG = HEADS * VD
EXT = MSG + 128

HALF = 80
FOUR = 4 * PER
FULL = FOUR + 32

EARLY = [(0, 0)] + [(o, s) for s in (1, 2) for o in (0, 1)]
LATE = [(0, 3), (1, 3), (0, 4)]
CHUNKS = EARLY + LATE
PIECES = [(j % 2, o, s, j // 2) for o, s in CHUNKS for j in range(4)]
SLOTS = len(PIECES)
KEYS = SLOTS * PER

VAT = 256
QT = 256
KT = FOUR
SMALL = pltpu.CompilerParams(vmem_limit_bytes=8 * 1024 * 1024)


def attend_kernel(count, first, *refs):
    chunks, refs = refs[:count], refs[count:]
    if first:
        q_ref, w_ref, thr_ref, old_ref, lse_ref, o_ref, kv, sco = refs
    else:
        q_ref, w_ref, thr_ref, o_ref, lse_ref, kv, sco = refs
    units = [(h, t) for h in range(HEADS) for t in range(ROWS // QT)]
    off = lax.broadcasted_iota(jnp.int32, (64, 128), 0).astype(jnp.float32)
    lane = lax.broadcasted_iota(jnp.int32, (QT, 128), 1)

    def project(h, c):
        new = jnp.dot(chunks[c][0:FOUR, :], w_ref[h], preferred_element_type=jnp.float32)
        new = new.astype(jnp.bfloat16)
        rows = slice(c * FOUR, (c + 1) * FOUR)
        kv[h % 2, rows, 0:QN] = new[:, 0:QN]
        kv[h % 2, rows, VAT:] = new[:, QN:]

    for c in range(count):
        for r in range(FOUR // 16):
            at = FOUR + 16 * (r // 8)
            rope = chunks[c][at : at + 16, (r % 8) * QR : (r % 8 + 1) * QR]
            for b in range(2):
                kv[b, c * FOUR + r * 16 : c * FOUR + (r + 1) * 16, QN:QD] = rope
        project(0, c)

    def score(u, i, top):
        h, t = units[u]
        q = q_ref[t * QT : (t + 1) * QT, h * QD : (h + 1) * QD]
        s = lax.dot_general(
            q,
            kv[h % 2, i * KT : (i + 1) * KT, 0:QD],
            (((1,), (1,)), ((), ())),
            preferred_element_type=jnp.float32,
        )
        parts = []
        for b in range(QT // 64):
            row = t * (QT // 64) + b
            at = (first + i) * KT
            thr = thr_ref[row : row + 1, at : at + KT]
            cols = []
            for c in range(KT // 128):
                piece = s[b * 64 : (b + 1) * 64, c * 128 : (c + 1) * 128]
                cols.append(jnp.where(off >= thr[:, c * 128 : (c + 1) * 128], piece, NEG))
            parts.append(functools.reduce(jnp.maximum, cols))
            for c in range(KT // 128):
                at = i * KT + c * 128
                sco[u % 2, b * 64 : (b + 1) * 64, at : at + 128] = cols[c]
        best = jnp.concatenate(parts, axis=0)
        return best if top is None else jnp.maximum(top, best)

    def mix(u, i, mc, total, acc):
        h, t = units[u]
        p = jnp.exp2(sco[u % 2, :, i * KT : (i + 1) * KT] * (SCALE * LOG2E) - mc)
        for c in range(KT // 128):
            piece = p[:, c * 128 : (c + 1) * 128]
            total = piece if total is None else total + piece
        new = jnp.dot(
            p.astype(jnp.bfloat16),
            kv[h % 2, i * KT : (i + 1) * KT, VAT:],
            preferred_element_type=jnp.float32,
        )
        return total, new if acc is None else acc + new

    stats = [jnp.zeros((QT, 128), jnp.float32) for _ in range(ROWS // QT)]
    m = None
    for u in range(len(units) + 1):
        top = total = acc = None
        if u:
            mc = m * (SCALE * LOG2E)
        for i in range(count):
            if u < len(units):
                top = score(u, i, top)
            if u:
                total, acc = mix(u - 1, i, mc, total, acc)
            if u < len(units):
                h, t = units[u]
                if t == ROWS // QT - 1 and h + 1 < HEADS:
                    project(h + 1, i)
        if u:
            h, t = units[u - 1]
            rows = slice(t * QT, (t + 1) * QT)
            den = jnp.sum(total, axis=1, keepdims=True)
            lse = m * SCALE + jnp.log(den)
            out = acc / den
            cols = slice(h * VD, (h + 1) * VD)
            if first:
                before = lse_ref[rows, h : h + 1]
                both = jnp.maximum(before, lse)
                part, rest = jnp.exp(lse - both), jnp.exp(before - both)
                out = (out * part + old_ref[rows, cols] * rest) / (part + rest)
                lse = both + jnp.log(part + rest)
                hi = lse.astype(jnp.bfloat16).astype(jnp.float32)
                mid = (lse - hi).astype(jnp.bfloat16).astype(jnp.float32)
                old = jnp.where(lane == 3 * h, hi, stats[t])
                old = jnp.where(lane == 3 * h + 1, mid, old)
                stats[t] = jnp.where(lane == 3 * h + 2, lse - hi - mid, old)
            else:
                stats[t] = jnp.where(lane == h, lse, stats[t])
            o_ref[rows, cols] = out.astype(o_ref.dtype)
        if u < len(units):
            m = jnp.max(top, axis=1, keepdims=True)
    for t in range(ROWS // QT):
        if first:
            o_ref[t * QT : (t + 1) * QT, MSG:] = stats[t].astype(jnp.bfloat16)
        else:
            lse_ref[t * QT : (t + 1) * QT, :] = stats[t]


def attend(chunks, q, weights, thr, before=()):
    count = len(chunks)
    first = len(CHUNKS) - count if before else 0
    if before:
        shape = jax.ShapeDtypeStruct((ROWS, EXT), jnp.bfloat16)
    else:
        shape = (
            jax.ShapeDtypeStruct((ROWS, MSG), jnp.float32),
            jax.ShapeDtypeStruct((ROWS, 128), jnp.float32),
        )
    return pl.pallas_call(
        functools.partial(attend_kernel, count, first),
        out_shape=shape,
        scratch_shapes=[
            pltpu.VMEM((2, count * FOUR, VAT + VD), jnp.bfloat16),
            pltpu.VMEM((2, QT, count * FOUR), jnp.float32),
        ],
        compiler_params=pltpu.CompilerParams(vmem_limit_bytes=24 * 1024 * 1024),
        cost_estimate=pl.CostEstimate(
            flops=1_000_000 * count, bytes_accessed=1_000 * count, transcendentals=1_000 * count
        ),
        name="attend_late" if before else "attend_early",
    )(*chunks, q, weights, thr, *before)


def combine_kernel(x_ref, o_ref):
    n = GRP * TOK
    ext = [x_ref[pl.ds(c * n, n), MSG:].astype(jnp.float32) for c in range(CELLS)]
    for h in range(HEADS):
        j = 3 * h
        lse = [e[:, j : j + 1] + e[:, j + 1 : j + 2] + e[:, j + 2 : j + 3] for e in ext]
        top = functools.reduce(jnp.maximum, lse)
        part = [jnp.exp(v - top) for v in lse]
        scale = 1.0 / functools.reduce(jnp.add, part)
        acc = jnp.zeros((n, VD), jnp.float32)
        for c in range(CELLS):
            acc = acc + x_ref[pl.ds(c * n, n), pl.ds(h * VD, VD)].astype(jnp.float32) * (
                part[c] * scale
            )
        o_ref[:, :, pl.ds(h * VD, VD)] = acc.reshape(GRP, TOK, VD).astype(jnp.bfloat16)


def combine(x):
    return pl.pallas_call(
        combine_kernel,
        out_shape=jax.ShapeDtypeStruct((GRP, TOK, MSG), jnp.bfloat16),
        compiler_params=SMALL,
        name="combine",
    )(x)


def pack_kernel(lat_ref, rope_ref, o_ref):
    o_ref[0:PER, :] = lat_ref[...]
    for r in range(L // QR):
        b = r % (PER // 16)
        o_ref[PER:HALF, r * QR : (r + 1) * QR] = rope_ref[b * 16 : (b + 1) * 16, :]


def pack(latents, key_rope):
    return pl.pallas_call(
        pack_kernel,
        out_shape=jax.ShapeDtypeStruct((HALF, L), jnp.bfloat16),
        compiler_params=SMALL,
        name="pack",
    )(latents, key_rope)


def merge_kernel(*refs):
    o_ref = refs[-1]
    for j, ref in enumerate(refs[:-1]):
        half = slice(j % 2 * (L // 2), (j % 2 + 1) * (L // 2))
        at = FOUR + j // 2 * 16
        o_ref[j * PER : (j + 1) * PER, :] = ref[0:PER, :]
        o_ref[at : at + 16, half] = ref[PER:HALF, half]


def merge(pieces):
    return pl.pallas_call(
        merge_kernel,
        out_shape=jax.ShapeDtypeStruct((FULL, L), jnp.bfloat16),
        compiler_params=SMALL,
        name="merge",
    )(*pieces)


def shift(n, k):
    return [(i, (i + k) % n) for i in range(n)]


def gather_keys(latents, key_rope, swap):
    near = [(a * 2 + b, (1 - a) * 2 + 1 - b) for a in range(2) for b in range(2)]
    to_core = lambda x: lax.ppermute(x, "core", shift(CN, 1))

    def round_z(x, n):
        up = [(i, (i + n) % ZN) for i in range(ZN)]
        down = [(ZN + i, ZN + (i - n) % ZN) for i in range(ZN)]
        return lax.ppermute(x, ("core", "z"), up + down)

    piece = pack(latents, key_rope)
    beside, mate = lax.ppermute(piece, ("xl", "xh"), near), to_core(piece)
    pieces = [piece, beside, mate, to_core(beside)]
    mine = swap(mate)
    now = merge(pieces)
    got = {(0, 0): now, (0, 1): round_z(now, 1), (0, 2): round_z(now, 2)}
    got[0, 1], got[0, 2], mine = lax.optimization_barrier((got[0, 1], got[0, 2], mine))
    after = got[0, 2]
    got[0, 3] = round_z(after, 1)
    got[0, 4] = round_z(after, 2)
    for s in (1, 2):
        got[1, s] = to_core(got[0, s])
    return got, to_core, mine, beside


def threshold_kernel(pattern_ref, stripe_ref, o_ref):
    xl, y, core = lax.axis_index("xl"), lax.axis_index("y"), lax.axis_index("core")
    xh, z = lax.axis_index("xh"), lax.axis_index("z")
    lane = lax.broadcasted_iota(jnp.int32, (1, 128), 1)
    blocks = stripe_ref.shape[0]

    def facts(swap, other, step, inner):
        side = core ^ other
        zz = lax.rem(z + jnp.where(side == 1, step, ZN - step), ZN)
        cell = ((xl ^ swap) * YN + y) * CN + (side ^ inner)
        place = cell * GRP + (xh ^ swap) * ZN + zz
        return stripe_ref[lax.shift_right_logical(place, 1)], (place & 1) * PER - core * 64

    for pair in range(SLOTS // 2):
        two = [facts(*PIECES[2 * pair + j]) for j in range(2)]
        for r in range(CELLS):
            vals = []
            for j, (kb, base) in enumerate(two):
                see = (kb < blocks - CELLS + r) & (pattern_ref[r, kb] == 1)
                same = kb == blocks - CELLS + r
                const = jnp.where(see, -BLOCK, jnp.where(same, base - j * PER, 4 * BLOCK))
                vals.append(const + lane * jnp.where(same, 1, 0))
            row = jnp.where(lane < PER, vals[0], vals[1]).astype(jnp.float32)
            o_ref[r : r + 1, pair * 128 : (pair + 1) * 128] = row


def thresholds(pattern, stripe):
    return pl.pallas_call(
        threshold_kernel,
        out_shape=jax.ShapeDtypeStruct((CELLS, KEYS), jnp.float32),
        in_specs=[pl.BlockSpec(memory_space=pltpu.SMEM)] * 2,
        compiler_params=SMALL,
        name="thresholds",
    )(pattern, stripe)


def body(queries, latents, key_rope, key_up, value_up, pattern, stripe):
    cells = ("xl", "y")
    groups = ("xh", "z")
    def swap(after):
        send = queries.reshape(TOK, GRP, HEADS * QD).transpose(1, 0, 2)
        send, _ = lax.optimization_barrier((send, after))
        return lax.all_to_all(send, groups, split_axis=0, concat_axis=0, tiled=True)

    got, to_core, mine, mark = gather_keys(latents, key_rope, swap)
    mine = mine.reshape(GRP * TOK, HEADS * QD)
    send = jnp.broadcast_to(mine[None], (CELLS, *mine.shape))
    q = lax.all_to_all(send, cells, split_axis=0, concat_axis=0, tiled=True)
    q = q.reshape(ROWS, HEADS * QD)
    key_up, value_up, pattern, stripe, _ = lax.optimization_barrier(
        (key_up, value_up, pattern, stripe, mark)
    )
    weights = jnp.concatenate([key_up.transpose(0, 2, 1), value_up], axis=2)
    thr = thresholds(pattern, stripe)
    before = attend([got[c] for c in EARLY], q, weights, thr)
    (got[0, 3], got[0, 4]), before = lax.optimization_barrier(((got[0, 3], got[0, 4]), before))
    got[1, 3] = to_core(got[0, 3])
    part = attend([got[c] for c in LATE], q, weights, thr, before)
    back = lax.all_to_all(
        part.reshape(CELLS, GRP * TOK, EXT), cells, split_axis=0, concat_axis=0, tiled=True
    )
    out = lax.all_to_all(combine(back.reshape(ROWS, EXT)), groups, split_axis=0, concat_axis=0, tiled=True)
    return out.transpose(1, 0, 2).reshape(TOK, GRP * MSG)


def solution(mesh):
    fine = Mesh(mesh.devices.reshape(XLN, YN, CN, XHN, ZN), AXES)
    in_specs = (
        P(AXES, None),
        P(AXES, None),
        P(AXES, None),
        P(("xh", "z"), None, None),
        P(("xh", "z"), None, None),
        P(),
        P(),
    )
    return jax.shard_map(body, mesh=fine, in_specs=in_specs, out_specs=P(AXES, None), check_vma=False)
```

```python
import functools
import math

import jax
import jax.numpy as jnp
from jax import lax
from jax.experimental import pallas as pl
from jax.experimental.pallas import tpu as pltpu
from jax.sharding import Mesh
from jax.sharding import PartitionSpec as P

L = 512
QN = 128
QR = 64
QD = QN + QR
VD = 128
BLOCK = 128
HEADS = 4
NEG = -1e30
SCALE = 1.0 / math.sqrt(QD)
LOG2E = math.log2(math.e)

AXES = ("xl", "y", "core", "xh", "z")
XLN, YN, CN, XHN, ZN = 2, 4, 2, 2, 8
CELLS = XLN * YN
GRP = XHN * ZN
PER = 64
TOK = 4
ROWS = CELLS * GRP * TOK
MSG = HEADS * VD
EXT = MSG + 128

HALF = 80
FOUR = 4 * PER
FULL = FOUR + 32

EARLY = [(0, 0)] + [(o, s) for s in (1, 2) for o in (0, 1)]
LATE = [(0, 3), (1, 3), (0, 4), (1, 4)]
PIECES = [(j % 2, o, s, j // 2) for o, s in EARLY + LATE for j in range(4 if s < 4 else 2)]
SLOTS = len(PIECES)
KEYS = SLOTS * PER

VAT = 256
QT = 256
KT = FOUR
SMALL = pltpu.CompilerParams(vmem_limit_bytes=8 * 1024 * 1024)


def attend_kernel(count, first, *refs):
    if first:
        chunks, halves, refs = refs[: count - 1], refs[count - 1 : count + 1], refs[count + 1 :]
        q_ref, w_ref, thr_ref, old_ref, lse_ref, o_ref, kv, sco, pair = refs
        for j, ref in enumerate(halves):
            pair[j * 2 * PER : (j + 1) * 2 * PER, :] = ref[0 : 2 * PER, :]
            pair[FOUR + j * 16 : FOUR + (j + 1) * 16, :] = ref[2 * PER :, :]
        chunks = (*chunks, pair)
    else:
        chunks, refs = refs[:count], refs[count:]
        q_ref, w_ref, thr_ref, o_ref, lse_ref, kv, sco = refs
    units = [(h, t) for h in range(HEADS) for t in range(ROWS // QT)]
    off = lax.broadcasted_iota(jnp.int32, (64, 128), 0).astype(jnp.float32)
    lane = lax.broadcasted_iota(jnp.int32, (QT, 128), 1)

    def project(h, c):
        new = jnp.dot(chunks[c][0:FOUR, :], w_ref[h], preferred_element_type=jnp.float32)
        new = new.astype(jnp.bfloat16)
        rows = slice(c * FOUR, (c + 1) * FOUR)
        kv[h % 2, rows, 0:QN] = new[:, 0:QN]
        kv[h % 2, rows, VAT:] = new[:, QN:]

    for c in range(count):
        for r in range(FOUR // 16):
            at = FOUR + 16 * (r // 8)
            rope = chunks[c][at : at + 16, (r % 8) * QR : (r % 8 + 1) * QR]
            for b in range(2):
                kv[b, c * FOUR + r * 16 : c * FOUR + (r + 1) * 16, QN:QD] = rope
        project(0, c)

    def score(u, i, top):
        h, t = units[u]
        q = q_ref[t * QT : (t + 1) * QT, h * QD : (h + 1) * QD]
        s = lax.dot_general(
            q,
            kv[h % 2, i * KT : (i + 1) * KT, 0:QD],
            (((1,), (1,)), ((), ())),
            preferred_element_type=jnp.float32,
        )
        parts = []
        for b in range(QT // 64):
            row = t * (QT // 64) + b
            at = (first + i) * KT
            thr = thr_ref[row : row + 1, at : at + KT]
            cols = []
            for c in range(KT // 128):
                piece = s[b * 64 : (b + 1) * 64, c * 128 : (c + 1) * 128]
                cols.append(jnp.where(off >= thr[:, c * 128 : (c + 1) * 128], piece, NEG))
            parts.append(functools.reduce(jnp.maximum, cols))
            for c in range(KT // 128):
                at = i * KT + c * 128
                sco[u % 2, b * 64 : (b + 1) * 64, at : at + 128] = cols[c]
        best = jnp.concatenate(parts, axis=0)
        return best if top is None else jnp.maximum(top, best)

    def mix(u, i, mc, total, acc):
        h, t = units[u]
        p = jnp.exp2(sco[u % 2, :, i * KT : (i + 1) * KT] * (SCALE * LOG2E) - mc)
        for c in range(KT // 128):
            piece = p[:, c * 128 : (c + 1) * 128]
            total = piece if total is None else total + piece
        new = jnp.dot(
            p.astype(jnp.bfloat16),
            kv[h % 2, i * KT : (i + 1) * KT, VAT:],
            preferred_element_type=jnp.float32,
        )
        return total, new if acc is None else acc + new

    stats = [jnp.zeros((QT, 128), jnp.float32) for _ in range(ROWS // QT)]
    m = None
    for u in range(len(units) + 1):
        top = total = acc = None
        if u:
            mc = m * (SCALE * LOG2E)
        for i in range(count):
            if u < len(units):
                top = score(u, i, top)
            if u:
                total, acc = mix(u - 1, i, mc, total, acc)
            if u < len(units):
                h, t = units[u]
                if t == ROWS // QT - 1 and h + 1 < HEADS:
                    project(h + 1, i)
        if u:
            h, t = units[u - 1]
            rows = slice(t * QT, (t + 1) * QT)
            den = jnp.sum(total, axis=1, keepdims=True)
            lse = m * SCALE + jnp.log(den)
            out = acc / den
            cols = slice(h * VD, (h + 1) * VD)
            if first:
                before = lse_ref[rows, h : h + 1]
                both = jnp.maximum(before, lse)
                part, rest = jnp.exp(lse - both), jnp.exp(before - both)
                out = (out * part + old_ref[rows, cols] * rest) / (part + rest)
                lse = both + jnp.log(part + rest)
                hi = lse.astype(jnp.bfloat16).astype(jnp.float32)
                mid = (lse - hi).astype(jnp.bfloat16).astype(jnp.float32)
                old = jnp.where(lane == 3 * h, hi, stats[t])
                old = jnp.where(lane == 3 * h + 1, mid, old)
                stats[t] = jnp.where(lane == 3 * h + 2, lse - hi - mid, old)
            else:
                stats[t] = jnp.where(lane == h, lse, stats[t])
            o_ref[rows, cols] = out.astype(o_ref.dtype)
        if u < len(units):
            m = jnp.max(top, axis=1, keepdims=True)
    for t in range(ROWS // QT):
        if first:
            o_ref[t * QT : (t + 1) * QT, MSG:] = stats[t].astype(jnp.bfloat16)
        else:
            lse_ref[t * QT : (t + 1) * QT, :] = stats[t]


def attend(chunks, q, weights, thr, before=()):
    count = len(chunks) - 1 if before else len(chunks)
    first = len(EARLY) if before else 0
    scratch = [
        pltpu.VMEM((2, count * FOUR, VAT + VD), jnp.bfloat16),
        pltpu.VMEM((2, QT, count * FOUR), jnp.float32),
    ]
    if before:
        scratch.append(pltpu.VMEM((FULL, L), jnp.bfloat16))
        shape = jax.ShapeDtypeStruct((ROWS, EXT), jnp.bfloat16)
    else:
        shape = (
            jax.ShapeDtypeStruct((ROWS, MSG), jnp.float32),
            jax.ShapeDtypeStruct((ROWS, 128), jnp.float32),
        )
    return pl.pallas_call(
        functools.partial(attend_kernel, count, first),
        out_shape=shape,
        scratch_shapes=scratch,
        compiler_params=pltpu.CompilerParams(vmem_limit_bytes=24 * 1024 * 1024),
        cost_estimate=pl.CostEstimate(
            flops=1_000_000 * count, bytes_accessed=1_000 * count, transcendentals=1_000 * count
        ),
        name="attend_late" if before else "attend_early",
    )(*chunks, q, weights, thr, *before)


def combine_kernel(x_ref, o_ref):
    n = GRP * TOK
    ext = [x_ref[pl.ds(c * n, n), MSG:].astype(jnp.float32) for c in range(CELLS)]
    for h in range(HEADS):
        j = 3 * h
        lse = [e[:, j : j + 1] + e[:, j + 1 : j + 2] + e[:, j + 2 : j + 3] for e in ext]
        top = functools.reduce(jnp.maximum, lse)
        part = [jnp.exp(v - top) for v in lse]
        scale = 1.0 / functools.reduce(jnp.add, part)
        acc = jnp.zeros((n, VD), jnp.float32)
        for c in range(CELLS):
            acc = acc + x_ref[pl.ds(c * n, n), pl.ds(h * VD, VD)].astype(jnp.float32) * (
                part[c] * scale
            )
        o_ref[:, :, pl.ds(h * VD, VD)] = acc.reshape(GRP, TOK, VD).astype(jnp.bfloat16)


def combine(x):
    return pl.pallas_call(
        combine_kernel,
        out_shape=jax.ShapeDtypeStruct((GRP, TOK, MSG), jnp.bfloat16),
        compiler_params=SMALL,
        name="combine",
    )(x)


def pack_kernel(lat_ref, rope_ref, o_ref):
    o_ref[0:PER, :] = lat_ref[...]
    for r in range(L // QR):
        b = r % (PER // 16)
        o_ref[PER:HALF, r * QR : (r + 1) * QR] = rope_ref[b * 16 : (b + 1) * 16, :]


def pack(latents, key_rope):
    return pl.pallas_call(
        pack_kernel,
        out_shape=jax.ShapeDtypeStruct((HALF, L), jnp.bfloat16),
        compiler_params=SMALL,
        name="pack",
    )(latents, key_rope)


def merge_kernel(*refs):
    o_ref = refs[-1]
    for j, ref in enumerate(refs[:-1]):
        half = slice(j % 2 * (L // 2), (j % 2 + 1) * (L // 2))
        at = FOUR + j // 2 * 16
        o_ref[j * PER : (j + 1) * PER, :] = ref[0:PER, :]
        o_ref[at : at + 16, half] = ref[PER:HALF, half]


def merge(pieces):
    return pl.pallas_call(
        merge_kernel,
        out_shape=jax.ShapeDtypeStruct((FULL, L), jnp.bfloat16),
        compiler_params=SMALL,
        name="merge",
    )(*pieces)


def halve_kernel(x_ref, o_ref):
    o_ref[0 : 2 * PER, :] = x_ref[0 : 2 * PER, :]
    o_ref[2 * PER :, :] = x_ref[FOUR : FOUR + 16, :]


def halve(chunk):
    return pl.pallas_call(
        halve_kernel,
        out_shape=jax.ShapeDtypeStruct((FULL // 2, L), jnp.bfloat16),
        compiler_params=SMALL,
        name="halve",
    )(chunk)


def shift(n, k):
    return [(i, (i + k) % n) for i in range(n)]


def gather_keys(latents, key_rope, swap, prepare):
    near = [(a * 2 + b, (1 - a) * 2 + 1 - b) for a in range(2) for b in range(2)]
    to_core = lambda x: lax.ppermute(x, "core", shift(CN, 1))

    def round_z(x, n):
        up = [(i, (i + n) % ZN) for i in range(ZN)]
        down = [(ZN + i, ZN + (i - n) % ZN) for i in range(ZN)]
        return lax.ppermute(x, ("core", "z"), up + down)

    piece = pack(latents, key_rope)
    beside, mate = lax.ppermute(piece, ("xl", "xh"), near), to_core(piece)
    mine = swap(beside)
    pieces = [piece, beside, mate, to_core(beside)]
    pieces, mine = lax.optimization_barrier((pieces, mine))
    now = merge(pieces)
    got = {(0, 0): now, (0, 1): round_z(now, 1), (0, 2): round_z(now, 2)}
    got[0, 2], extra = lax.optimization_barrier((got[0, 2], prepare(beside)))
    got[0, 3] = round_z(got[0, 2], 1)
    got[0, 4] = round_z(halve(got[0, 2]), 2)
    for s in (1, 2):
        got[1, s] = to_core(got[0, s])
    mine, _ = lax.optimization_barrier((mine, now))
    return got, to_core, mine, extra


def threshold_kernel(pattern_ref, stripe_ref, o_ref):
    xl, y, core = lax.axis_index("xl"), lax.axis_index("y"), lax.axis_index("core")
    xh, z = lax.axis_index("xh"), lax.axis_index("z")
    lane = lax.broadcasted_iota(jnp.int32, (1, 128), 1)
    blocks = stripe_ref.shape[0]

    def facts(swap, other, step, inner):
        side = core ^ other
        zz = lax.rem(z + jnp.where(side == 1, step, ZN - step), ZN)
        cell = ((xl ^ swap) * YN + y) * CN + (side ^ inner)
        place = cell * GRP + (xh ^ swap) * ZN + zz
        return stripe_ref[lax.shift_right_logical(place, 1)], (place & 1) * PER - core * 64

    for pair in range(SLOTS // 2):
        two = [facts(*PIECES[2 * pair + j]) for j in range(2)]
        for r in range(CELLS):
            vals = []
            for j, (kb, base) in enumerate(two):
                see = (kb < blocks - CELLS + r) & (pattern_ref[r, kb] == 1)
                same = kb == blocks - CELLS + r
                const = jnp.where(see, -BLOCK, jnp.where(same, base - j * PER, 4 * BLOCK))
                vals.append(const + lane * jnp.where(same, 1, 0))
            row = jnp.where(lane < PER, vals[0], vals[1]).astype(jnp.float32)
            o_ref[r : r + 1, pair * 128 : (pair + 1) * 128] = row


def thresholds(pattern, stripe):
    return pl.pallas_call(
        threshold_kernel,
        out_shape=jax.ShapeDtypeStruct((CELLS, KEYS), jnp.float32),
        in_specs=[pl.BlockSpec(memory_space=pltpu.SMEM)] * 2,
        compiler_params=SMALL,
        name="thresholds",
    )(pattern, stripe)


def body(queries, latents, key_rope, key_up, value_up, pattern, stripe):
    cells = ("xl", "y")
    groups = ("xh", "z")
    def swap(after):
        send = queries.reshape(TOK, GRP, HEADS * QD).transpose(1, 0, 2)
        send, _ = lax.optimization_barrier((send, after))
        return lax.all_to_all(send, groups, split_axis=0, concat_axis=0, tiled=True)

    def prepare(after):
        up, down, seen, order, _ = lax.optimization_barrier(
            (key_up, value_up, pattern, stripe, after)
        )
        weights = jnp.concatenate([up.transpose(0, 2, 1), down], axis=2)
        return weights, thresholds(seen, order)

    got, to_core, mine, (weights, thr) = gather_keys(latents, key_rope, swap, prepare)
    mine = mine.reshape(GRP * TOK, HEADS * QD)
    send = jnp.broadcast_to(mine[None], (CELLS, *mine.shape))
    q = lax.all_to_all(send, cells, split_axis=0, concat_axis=0, tiled=True)
    q = q.reshape(ROWS, HEADS * QD)
    before = attend([got[c] for c in EARLY], q, weights, thr)
    (got[0, 3], got[0, 4]), before = lax.optimization_barrier(((got[0, 3], got[0, 4]), before))
    for s in (3, 4):
        got[1, s] = to_core(got[0, s])
    part = attend([got[c] for c in LATE], q, weights, thr, before)
    back = lax.all_to_all(
        part.reshape(CELLS, GRP * TOK, EXT), cells, split_axis=0, concat_axis=0, tiled=True
    )
    out = lax.all_to_all(combine(back.reshape(ROWS, EXT)), groups, split_axis=0, concat_axis=0, tiled=True)
    return out.transpose(1, 0, 2).reshape(TOK, GRP * MSG)


def solution(mesh):
    fine = Mesh(mesh.devices.reshape(XLN, YN, CN, XHN, ZN), AXES)
    in_specs = (
        P(AXES, None),
        P(AXES, None),
        P(AXES, None),
        P(("xh", "z"), None, None),
        P(("xh", "z"), None, None),
        P(),
        P(),
    )
    return jax.shard_map(body, mesh=fine, in_specs=in_specs, out_specs=P(AXES, None), check_vma=False)
```

```python
import functools
import math

import jax
import jax.numpy as jnp
from jax import lax
from jax.experimental import pallas as pl
from jax.experimental.pallas import tpu as pltpu
from jax.sharding import Mesh
from jax.sharding import PartitionSpec as P

L = 512
QN = 128
QR = 64
QD = QN + QR
VD = 128
BLOCK = 128
HEADS = 4
NEG = -1e30
SCALE = 1.0 / math.sqrt(QD)
LOG2E = math.log2(math.e)

CHIPS = ("xl", "y", "xh", "z")
AXES = ("xl", "y", "core", "xh", "z")
XLN, YN, CN, XHN, ZN = 2, 4, 2, 2, 8
CELLS = XLN * YN
GRP = XHN * ZN
PER = 64
TOK = 4
ROWS = CELLS * GRP * TOK
MSG = HEADS * VD
EXT = MSG + 128

HALF = 80
FOUR = 4 * PER
FULL = FOUR + 32

EARLY = [(0, 0)] + [(o, s) for s in (1, 2) for o in (0, 1)]
LATE = [(0, 3), (1, 3), (0, 4), (1, 4)]
PIECES = [(j % 2, o, s, j // 2) for o, s in EARLY + LATE for j in range(4 if s < 4 else 2)]
SLOTS = len(PIECES)
KEYS = SLOTS * PER

VAT = 256
QT = 256
KT = FOUR
SMALL = pltpu.CompilerParams(vmem_limit_bytes=8 * 1024 * 1024)


def attend_kernel(count, first, *refs):
    if first:
        chunks, halves, refs = refs[: count - 1], refs[count - 1 : count + 1], refs[count + 1 :]
        q_ref, w_ref, thr_ref, old_ref, lse_ref, o_ref, kv, sco, pair = refs
        for j, ref in enumerate(halves):
            pair[j * 2 * PER : (j + 1) * 2 * PER, :] = ref[0 : 2 * PER, :]
            pair[FOUR + j * 16 : FOUR + (j + 1) * 16, :] = ref[2 * PER :, :]
        chunks = (*chunks, pair)
    else:
        chunks, refs = refs[:count], refs[count:]
        q_ref, w_ref, thr_ref, o_ref, lse_ref, kv, sco = refs
    units = [(h, t) for h in range(HEADS) for t in range(ROWS // QT)]
    off = lax.broadcasted_iota(jnp.int32, (64, 128), 0).astype(jnp.float32)
    lane = lax.broadcasted_iota(jnp.int32, (QT, 128), 1)

    def project(h, c):
        new = jnp.dot(chunks[c][0:FOUR, :], w_ref[h], preferred_element_type=jnp.float32)
        new = new.astype(jnp.bfloat16)
        rows = slice(c * FOUR, (c + 1) * FOUR)
        kv[h % 2, rows, 0:QN] = new[:, 0:QN]
        kv[h % 2, rows, VAT:] = new[:, QN:]

    for c in range(count):
        for r in range(FOUR // 16):
            at = FOUR + 16 * (r // 8)
            rope = chunks[c][at : at + 16, (r % 8) * QR : (r % 8 + 1) * QR]
            for b in range(2):
                kv[b, c * FOUR + r * 16 : c * FOUR + (r + 1) * 16, QN:QD] = rope
        project(0, c)

    def score(u, i, top):
        h, t = units[u]
        q = q_ref[t * QT : (t + 1) * QT, h * QD : (h + 1) * QD]
        s = lax.dot_general(
            q,
            kv[h % 2, i * KT : (i + 1) * KT, 0:QD],
            (((1,), (1,)), ((), ())),
            preferred_element_type=jnp.float32,
        )
        parts = []
        for b in range(QT // 64):
            row = t * (QT // 64) + b
            at = (first + i) * KT
            thr = thr_ref[row : row + 1, at : at + KT]
            cols = []
            for c in range(KT // 128):
                piece = s[b * 64 : (b + 1) * 64, c * 128 : (c + 1) * 128]
                cols.append(jnp.where(off >= thr[:, c * 128 : (c + 1) * 128], piece, NEG))
            parts.append(functools.reduce(jnp.maximum, cols))
            for c in range(KT // 128):
                at = i * KT + c * 128
                sco[u % 2, b * 64 : (b + 1) * 64, at : at + 128] = cols[c]
        best = jnp.concatenate(parts, axis=0)
        return best if top is None else jnp.maximum(top, best)

    def mix(u, i, mc, total, acc):
        h, t = units[u]
        p = jnp.exp2(sco[u % 2, :, i * KT : (i + 1) * KT] * (SCALE * LOG2E) - mc)
        for c in range(KT // 128):
            piece = p[:, c * 128 : (c + 1) * 128]
            total = piece if total is None else total + piece
        new = jnp.dot(
            p.astype(jnp.bfloat16),
            kv[h % 2, i * KT : (i + 1) * KT, VAT:],
            preferred_element_type=jnp.float32,
        )
        return total, new if acc is None else acc + new

    stats = [jnp.zeros((QT, 128), jnp.float32) for _ in range(ROWS // QT)]
    m = None
    for u in range(len(units) + 1):
        top = total = acc = None
        if u:
            mc = m * (SCALE * LOG2E)
        for i in range(count):
            if u < len(units):
                top = score(u, i, top)
            if u:
                total, acc = mix(u - 1, i, mc, total, acc)
            if u < len(units):
                h, t = units[u]
                if t == ROWS // QT - 1 and h + 1 < HEADS:
                    project(h + 1, i)
        if u:
            h, t = units[u - 1]
            rows = slice(t * QT, (t + 1) * QT)
            den = jnp.sum(total, axis=1, keepdims=True)
            lse = m * SCALE + jnp.log(den)
            out = acc / den
            cols = slice(h * VD, (h + 1) * VD)
            if first:
                before = lse_ref[rows, h : h + 1]
                both = jnp.maximum(before, lse)
                part, rest = jnp.exp(lse - both), jnp.exp(before - both)
                out = (out * part + old_ref[rows, cols] * rest) / (part + rest)
                lse = both + jnp.log(part + rest)
                hi = lse.astype(jnp.bfloat16).astype(jnp.float32)
                mid = (lse - hi).astype(jnp.bfloat16).astype(jnp.float32)
                old = jnp.where(lane == 3 * h, hi, stats[t])
                old = jnp.where(lane == 3 * h + 1, mid, old)
                stats[t] = jnp.where(lane == 3 * h + 2, lse - hi - mid, old)
            else:
                stats[t] = jnp.where(lane == h, lse, stats[t])
            o_ref[rows, cols] = out.astype(o_ref.dtype)
        if u < len(units):
            m = jnp.max(top, axis=1, keepdims=True)
    for t in range(ROWS // QT):
        if first:
            o_ref[t * QT : (t + 1) * QT, MSG:] = stats[t].astype(jnp.bfloat16)
        else:
            lse_ref[t * QT : (t + 1) * QT, :] = stats[t]


def attend(chunks, q, weights, thr, before=()):
    count = len(chunks) - 1 if before else len(chunks)
    first = len(EARLY) if before else 0
    scratch = [
        pltpu.VMEM((2, count * FOUR, VAT + VD), jnp.bfloat16),
        pltpu.VMEM((2, QT, count * FOUR), jnp.float32),
    ]
    if before:
        scratch.append(pltpu.VMEM((FULL, L), jnp.bfloat16))
        shape = jax.ShapeDtypeStruct((ROWS, EXT), jnp.bfloat16)
    else:
        shape = (
            jax.ShapeDtypeStruct((ROWS, MSG), jnp.float32),
            jax.ShapeDtypeStruct((ROWS, 128), jnp.float32),
        )
    return pl.pallas_call(
        functools.partial(attend_kernel, count, first),
        out_shape=shape,
        scratch_shapes=scratch,
        compiler_params=pltpu.CompilerParams(vmem_limit_bytes=24 * 1024 * 1024),
        cost_estimate=pl.CostEstimate(
            flops=1_000_000 * count, bytes_accessed=1_000 * count, transcendentals=1_000 * count
        ),
        name="attend_late" if before else "attend_early",
    )(*chunks, q, weights, thr, *before)


def combine_kernel(x_ref, o_ref):
    n = GRP * TOK
    ext = [x_ref[pl.ds(c * n, n), MSG:].astype(jnp.float32) for c in range(CELLS)]
    for h in range(HEADS):
        j = 3 * h
        lse = [e[:, j : j + 1] + e[:, j + 1 : j + 2] + e[:, j + 2 : j + 3] for e in ext]
        top = functools.reduce(jnp.maximum, lse)
        part = [jnp.exp(v - top) for v in lse]
        scale = 1.0 / functools.reduce(jnp.add, part)
        acc = jnp.zeros((n, VD), jnp.float32)
        for c in range(CELLS):
            acc = acc + x_ref[pl.ds(c * n, n), pl.ds(h * VD, VD)].astype(jnp.float32) * (
                part[c] * scale
            )
        o_ref[:, :, pl.ds(h * VD, VD)] = acc.reshape(GRP, TOK, VD).astype(jnp.bfloat16)


def combine(x):
    return pl.pallas_call(
        combine_kernel,
        out_shape=jax.ShapeDtypeStruct((GRP, TOK, MSG), jnp.bfloat16),
        compiler_params=SMALL,
        name="combine",
    )(x)


def pack_kernel(lat_ref, rope_ref, o_ref):
    o_ref[0:PER, :] = lat_ref[...]
    for r in range(L // QR):
        b = r % (PER // 16)
        o_ref[PER:HALF, r * QR : (r + 1) * QR] = rope_ref[b * 16 : (b + 1) * 16, :]


def pack(latents, key_rope):
    return pl.pallas_call(
        pack_kernel,
        out_shape=jax.ShapeDtypeStruct((HALF, L), jnp.bfloat16),
        compiler_params=SMALL,
        name="pack",
    )(latents, key_rope)


def merge_kernel(*refs):
    o_ref = refs[-1]
    for j, ref in enumerate(refs[:-1]):
        half = slice(j % 2 * (L // 2), (j % 2 + 1) * (L // 2))
        at = FOUR + j // 2 * 16
        o_ref[j * PER : (j + 1) * PER, :] = ref[0:PER, :]
        o_ref[at : at + 16, half] = ref[PER:HALF, half]


def merge(pieces):
    return pl.pallas_call(
        merge_kernel,
        out_shape=jax.ShapeDtypeStruct((FULL, L), jnp.bfloat16),
        compiler_params=SMALL,
        name="merge",
    )(*pieces)


def halve_kernel(x_ref, o_ref):
    o_ref[0 : 2 * PER, :] = x_ref[0 : 2 * PER, :]
    o_ref[2 * PER :, :] = x_ref[FOUR : FOUR + 16, :]


def halve(chunk):
    return pl.pallas_call(
        halve_kernel,
        out_shape=jax.ShapeDtypeStruct((FULL // 2, L), jnp.bfloat16),
        compiler_params=SMALL,
        name="halve",
    )(chunk)


def shift(n, k):
    return [(i, (i + k) % n) for i in range(n)]


def gather_keys(latents, key_rope, swap, prepare):
    near = [(a * 2 + b, (1 - a) * 2 + 1 - b) for a in range(2) for b in range(2)]
    to_core = lambda x: lax.ppermute(x, "core", shift(CN, 1))

    def round_z(x, n):
        up = [(i, (i + n) % ZN) for i in range(ZN)]
        down = [(ZN + i, ZN + (i - n) % ZN) for i in range(ZN)]
        return lax.ppermute(x, ("core", "z"), up + down)

    piece = pack(latents, key_rope)
    beside, mate = lax.ppermute(piece, ("xl", "xh"), near), to_core(piece)
    pieces = [piece, beside, mate, to_core(beside)]
    now = merge(pieces)
    mine = swap(now)
    got = {(0, 0): now, (0, 1): round_z(now, 1), (0, 2): round_z(now, 2)}
    got[0, 1], got[0, 2], extra = lax.optimization_barrier((got[0, 1], got[0, 2], prepare(beside)))
    got[0, 3] = round_z(got[0, 2], 1)
    got[0, 4] = round_z(halve(got[0, 2]), 2)
    for s in (1, 2):
        got[1, s] = to_core(got[0, s])
    return got, to_core, mine, extra


def threshold_kernel(pattern_ref, stripe_ref, o_ref):
    xl, y, core = lax.axis_index("xl"), lax.axis_index("y"), lax.axis_index("core")
    xh, z = lax.axis_index("xh"), lax.axis_index("z")
    lane = lax.broadcasted_iota(jnp.int32, (1, 128), 1)
    blocks = stripe_ref.shape[0]

    def facts(swap, other, step, inner):
        side = core ^ other
        zz = lax.rem(z + jnp.where(side == 1, step, ZN - step), ZN)
        cell = ((xl ^ swap) * YN + y) * CN + (side ^ inner)
        place = cell * GRP + (xh ^ swap) * ZN + zz
        return stripe_ref[lax.shift_right_logical(place, 1)], (place & 1) * PER - core * 64

    for pair in range(SLOTS // 2):
        two = [facts(*PIECES[2 * pair + j]) for j in range(2)]
        for r in range(CELLS):
            vals = []
            for j, (kb, base) in enumerate(two):
                see = (kb < blocks - CELLS + r) & (pattern_ref[r, kb] == 1)
                same = kb == blocks - CELLS + r
                const = jnp.where(see, -BLOCK, jnp.where(same, base - j * PER, 4 * BLOCK))
                vals.append(const + lane * jnp.where(same, 1, 0))
            row = jnp.where(lane < PER, vals[0], vals[1]).astype(jnp.float32)
            o_ref[r : r + 1, pair * 128 : (pair + 1) * 128] = row


def thresholds(pattern, stripe):
    return pl.pallas_call(
        threshold_kernel,
        out_shape=jax.ShapeDtypeStruct((CELLS, KEYS), jnp.float32),
        in_specs=[pl.BlockSpec(memory_space=pltpu.SMEM)] * 2,
        compiler_params=SMALL,
        name="thresholds",
    )(pattern, stripe)


def body(queries, latents, key_rope, key_up, value_up, pattern, stripe):
    cells = ("xl", "y")
    groups = ("xh", "z")
    def swap(after):
        send = queries.reshape(TOK, GRP, HEADS * QD).transpose(1, 0, 2)
        send, _ = lax.optimization_barrier((send, after))
        send = jnp.broadcast_to(send[None], (CELLS, *send.shape))
        send = send.reshape(CELLS * GRP, TOK, HEADS * QD)
        return lax.all_to_all(send, CHIPS, split_axis=0, concat_axis=0, tiled=True)

    def prepare(after):
        up, down, seen, order, _ = lax.optimization_barrier(
            (key_up, value_up, pattern, stripe, after)
        )
        weights = jnp.concatenate([up.transpose(0, 2, 1), down], axis=2)
        return weights, thresholds(seen, order)

    got, to_core, mine, (weights, thr) = gather_keys(latents, key_rope, swap, prepare)
    q = mine.reshape(ROWS, HEADS * QD)
    before = attend([got[c] for c in EARLY], q, weights, thr)
    (got[0, 3], got[0, 4]), before = lax.optimization_barrier(((got[0, 3], got[0, 4]), before))
    for s in (3, 4):
        got[1, s] = to_core(got[0, s])
    part = attend([got[c] for c in LATE], q, weights, thr, before)
    back = lax.all_to_all(
        part.reshape(CELLS, GRP * TOK, EXT), cells, split_axis=0, concat_axis=0, tiled=True
    )
    out = lax.all_to_all(combine(back.reshape(ROWS, EXT)), groups, split_axis=0, concat_axis=0, tiled=True)
    return out.transpose(1, 0, 2).reshape(TOK, GRP * MSG)


def solution(mesh):
    fine = Mesh(mesh.devices.reshape(XLN, YN, CN, XHN, ZN), AXES)
    in_specs = (
        P(AXES, None),
        P(AXES, None),
        P(AXES, None),
        P(("xh", "z"), None, None),
        P(("xh", "z"), None, None),
        P(),
        P(),
    )
    return jax.shard_map(body, mesh=fine, in_specs=in_specs, out_specs=P(AXES, None), check_vma=False)
```

```python
import functools
import math

import jax
import jax.numpy as jnp
from jax import lax
from jax.experimental import pallas as pl
from jax.experimental.pallas import tpu as pltpu
from jax.sharding import Mesh
from jax.sharding import PartitionSpec as P

L = 512
QN = 128
QR = 64
QD = QN + QR
VD = 128
BLOCK = 128
HEADS = 4
NEG = -1e30
SCALE = 1.0 / math.sqrt(QD)
LOG2E = math.log2(math.e)

AXES = ("xl", "y", "core", "xh", "z")
XLN, YN, CN, XHN, ZN = 2, 4, 2, 2, 8
CELLS = XLN * YN
GRP = XHN * ZN
PER = 64
TOK = 4
ROWS = CELLS * GRP * TOK
MSG = HEADS * VD
EXT = MSG + 128

HALF = 80
FOUR = 4 * PER
FULL = FOUR + 32

EARLY = [(0, 0)] + [(o, s) for s in (1, 2) for o in (0, 1)]
LATE = [(0, 3), (1, 3), (0, 4), (1, 4)]
PIECES = [(j % 2, o, s, j // 2) for o, s in EARLY + LATE for j in range(4 if s < 4 else 2)]
SLOTS = len(PIECES)
KEYS = SLOTS * PER

VAT = 256
QT = 256
KT = FOUR
SMALL = pltpu.CompilerParams(vmem_limit_bytes=8 * 1024 * 1024)


def attend_kernel(count, first, *refs):
    if first:
        chunks, halves, refs = refs[: count - 1], refs[count - 1 : count + 1], refs[count + 1 :]
        q_ref, w_ref, thr_ref, old_ref, lse_ref, o_ref, kv, sco, pair = refs
        for j, ref in enumerate(halves):
            pair[j * 2 * PER : (j + 1) * 2 * PER, :] = ref[0 : 2 * PER, :]
            pair[FOUR + j * 16 : FOUR + (j + 1) * 16, :] = ref[2 * PER :, :]
        chunks = (*chunks, pair)
    else:
        chunks, refs = refs[:count], refs[count:]
        q_ref, w_ref, thr_ref, o_ref, lse_ref, kv, sco = refs
    units = [(h, t) for h in range(HEADS) for t in range(ROWS // QT)]
    off = lax.broadcasted_iota(jnp.int32, (64, 128), 0).astype(jnp.float32)
    lane = lax.broadcasted_iota(jnp.int32, (QT, 128), 1)

    def project(h, c):
        new = jnp.dot(chunks[c][0:FOUR, :], w_ref[h], preferred_element_type=jnp.float32)
        new = new.astype(jnp.bfloat16)
        rows = slice(c * FOUR, (c + 1) * FOUR)
        kv[h % 2, rows, 0:QN] = new[:, 0:QN]
        kv[h % 2, rows, VAT:] = new[:, QN:]

    for c in range(count):
        for r in range(FOUR // 16):
            at = FOUR + 16 * (r // 8)
            rope = chunks[c][at : at + 16, (r % 8) * QR : (r % 8 + 1) * QR]
            for b in range(2):
                kv[b, c * FOUR + r * 16 : c * FOUR + (r + 1) * 16, QN:QD] = rope
        project(0, c)

    def score(u, i, top):
        h, t = units[u]
        q = q_ref[t * QT : (t + 1) * QT, h * QD : (h + 1) * QD]
        s = lax.dot_general(
            q,
            kv[h % 2, i * KT : (i + 1) * KT, 0:QD],
            (((1,), (1,)), ((), ())),
            preferred_element_type=jnp.float32,
        )
        parts = []
        for b in range(QT // 64):
            row = t * (QT // 64) + b
            at = (first + i) * KT
            thr = thr_ref[row : row + 1, at : at + KT]
            cols = []
            for c in range(KT // 128):
                piece = s[b * 64 : (b + 1) * 64, c * 128 : (c + 1) * 128]
                cols.append(jnp.where(off >= thr[:, c * 128 : (c + 1) * 128], piece, NEG))
            parts.append(functools.reduce(jnp.maximum, cols))
            for c in range(KT // 128):
                at = i * KT + c * 128
                sco[u % 2, b * 64 : (b + 1) * 64, at : at + 128] = cols[c]
        best = jnp.concatenate(parts, axis=0)
        return best if top is None else jnp.maximum(top, best)

    def mix(u, i, mc, total, acc):
        h, t = units[u]
        p = jnp.exp2(sco[u % 2, :, i * KT : (i + 1) * KT] * (SCALE * LOG2E) - mc)
        for c in range(KT // 128):
            piece = p[:, c * 128 : (c + 1) * 128]
            total = piece if total is None else total + piece
        new = jnp.dot(
            p.astype(jnp.bfloat16),
            kv[h % 2, i * KT : (i + 1) * KT, VAT:],
            preferred_element_type=jnp.float32,
        )
        return total, new if acc is None else acc + new

    stats = [jnp.zeros((QT, 128), jnp.float32) for _ in range(ROWS // QT)]
    m = None
    for u in range(len(units) + 1):
        top = total = acc = None
        if u:
            mc = m * (SCALE * LOG2E)
        for i in range(count):
            if u < len(units):
                top = score(u, i, top)
            if u:
                total, acc = mix(u - 1, i, mc, total, acc)
            if u < len(units):
                h, t = units[u]
                if t == ROWS // QT - 1 and h + 1 < HEADS:
                    project(h + 1, i)
        if u:
            h, t = units[u - 1]
            rows = slice(t * QT, (t + 1) * QT)
            den = jnp.sum(total, axis=1, keepdims=True)
            lse = m * SCALE + jnp.log(den)
            out = acc / den
            cols = slice(h * VD, (h + 1) * VD)
            if first:
                before = lse_ref[rows, h : h + 1]
                both = jnp.maximum(before, lse)
                part, rest = jnp.exp(lse - both), jnp.exp(before - both)
                out = (out * part + old_ref[rows, cols] * rest) / (part + rest)
                lse = both + jnp.log(part + rest)
                hi = lse.astype(jnp.bfloat16).astype(jnp.float32)
                mid = (lse - hi).astype(jnp.bfloat16).astype(jnp.float32)
                old = jnp.where(lane == 3 * h, hi, stats[t])
                old = jnp.where(lane == 3 * h + 1, mid, old)
                stats[t] = jnp.where(lane == 3 * h + 2, lse - hi - mid, old)
            else:
                stats[t] = jnp.where(lane == h, lse, stats[t])
            o_ref[rows, cols] = out.astype(o_ref.dtype)
        if u < len(units):
            m = jnp.max(top, axis=1, keepdims=True)
    for t in range(ROWS // QT):
        if first:
            o_ref[t * QT : (t + 1) * QT, MSG:] = stats[t].astype(jnp.bfloat16)
        else:
            lse_ref[t * QT : (t + 1) * QT, :] = stats[t]


def attend(chunks, q, weights, thr, before=()):
    count = len(chunks) - 1 if before else len(chunks)
    first = len(EARLY) if before else 0
    scratch = [
        pltpu.VMEM((2, count * FOUR, VAT + VD), jnp.bfloat16),
        pltpu.VMEM((2, QT, count * FOUR), jnp.float32),
    ]
    if before:
        scratch.append(pltpu.VMEM((FULL, L), jnp.bfloat16))
        shape = jax.ShapeDtypeStruct((ROWS, EXT), jnp.bfloat16)
    else:
        shape = (
            jax.ShapeDtypeStruct((ROWS, MSG), jnp.float32),
            jax.ShapeDtypeStruct((ROWS, 128), jnp.float32),
        )
    return pl.pallas_call(
        functools.partial(attend_kernel, count, first),
        out_shape=shape,
        scratch_shapes=scratch,
        compiler_params=pltpu.CompilerParams(vmem_limit_bytes=24 * 1024 * 1024),
        cost_estimate=pl.CostEstimate(
            flops=1_000_000 * count, bytes_accessed=1_000 * count, transcendentals=1_000 * count
        ),
        name="attend_late" if before else "attend_early",
    )(*chunks, q, weights, thr, *before)


def combine_kernel(x_ref, o_ref):
    n = GRP * TOK
    ext = [x_ref[pl.ds(c * n, n), MSG:].astype(jnp.float32) for c in range(CELLS)]
    for h in range(HEADS):
        j = 3 * h
        lse = [e[:, j : j + 1] + e[:, j + 1 : j + 2] + e[:, j + 2 : j + 3] for e in ext]
        top = functools.reduce(jnp.maximum, lse)
        part = [jnp.exp(v - top) for v in lse]
        scale = 1.0 / functools.reduce(jnp.add, part)
        acc = jnp.zeros((n, VD), jnp.float32)
        for c in range(CELLS):
            acc = acc + x_ref[pl.ds(c * n, n), pl.ds(h * VD, VD)].astype(jnp.float32) * (
                part[c] * scale
            )
        o_ref[:, :, pl.ds(h * VD, VD)] = acc.reshape(GRP, TOK, VD).astype(jnp.bfloat16)


def combine(x):
    return pl.pallas_call(
        combine_kernel,
        out_shape=jax.ShapeDtypeStruct((GRP, TOK, MSG), jnp.bfloat16),
        compiler_params=SMALL,
        name="combine",
    )(x)


def pack_kernel(lat_ref, rope_ref, o_ref):
    o_ref[0:PER, :] = lat_ref[...]
    for r in range(L // QR):
        b = r % (PER // 16)
        o_ref[PER:HALF, r * QR : (r + 1) * QR] = rope_ref[b * 16 : (b + 1) * 16, :]


def pack(latents, key_rope):
    return pl.pallas_call(
        pack_kernel,
        out_shape=jax.ShapeDtypeStruct((HALF, L), jnp.bfloat16),
        compiler_params=SMALL,
        name="pack",
    )(latents, key_rope)


def merge_kernel(*refs):
    o_ref = refs[-1]
    for j, ref in enumerate(refs[:-1]):
        half = slice(j % 2 * (L // 2), (j % 2 + 1) * (L // 2))
        at = FOUR + j // 2 * 16
        o_ref[j * PER : (j + 1) * PER, :] = ref[0:PER, :]
        o_ref[at : at + 16, half] = ref[PER:HALF, half]


def merge(pieces):
    return pl.pallas_call(
        merge_kernel,
        out_shape=jax.ShapeDtypeStruct((FULL, L), jnp.bfloat16),
        compiler_params=SMALL,
        name="merge",
    )(*pieces)


def halve_kernel(x_ref, o_ref):
    o_ref[0 : 2 * PER, :] = x_ref[0 : 2 * PER, :]
    o_ref[2 * PER :, :] = x_ref[FOUR : FOUR + 16, :]


def halve(chunk):
    return pl.pallas_call(
        halve_kernel,
        out_shape=jax.ShapeDtypeStruct((FULL // 2, L), jnp.bfloat16),
        compiler_params=SMALL,
        name="halve",
    )(chunk)


def shift(n, k):
    return [(i, (i + k) % n) for i in range(n)]


def gather_keys(latents, key_rope, swap, prepare):
    near = [(a * 2 + b, (1 - a) * 2 + 1 - b) for a in range(2) for b in range(2)]
    to_core = lambda x: lax.ppermute(x, "core", shift(CN, 1))

    def round_z(x, n):
        up = [(i, (i + n) % ZN) for i in range(ZN)]
        down = [(ZN + i, ZN + (i - n) % ZN) for i in range(ZN)]
        return lax.ppermute(x, ("core", "z"), up + down)

    piece = pack(latents, key_rope)
    beside, mate = lax.ppermute(piece, ("xl", "xh"), near), to_core(piece)
    mine = swap(piece)
    pieces = [piece, beside, mate, to_core(beside)]
    pieces, mine = lax.optimization_barrier((pieces, mine))
    now = merge(pieces)
    got = {(0, 0): now, (0, 1): round_z(now, 1), (0, 2): round_z(now, 2)}
    got[0, 2], extra = lax.optimization_barrier((got[0, 2], prepare(beside)))
    got[0, 3] = round_z(got[0, 2], 1)
    got[0, 4] = round_z(halve(got[0, 2]), 2)
    for s in (1, 2):
        got[1, s] = to_core(got[0, s])
    mine, _ = lax.optimization_barrier((mine, now))
    return got, to_core, mine, extra


def threshold_kernel(pattern_ref, stripe_ref, o_ref):
    xl, y, core = lax.axis_index("xl"), lax.axis_index("y"), lax.axis_index("core")
    xh, z = lax.axis_index("xh"), lax.axis_index("z")
    lane = lax.broadcasted_iota(jnp.int32, (1, 128), 1)
    blocks = stripe_ref.shape[0]

    def facts(swap, other, step, inner):
        side = core ^ other
        zz = lax.rem(z + jnp.where(side == 1, step, ZN - step), ZN)
        cell = ((xl ^ swap) * YN + y) * CN + (side ^ inner)
        place = cell * GRP + (xh ^ swap) * ZN + zz
        return stripe_ref[lax.shift_right_logical(place, 1)], (place & 1) * PER - core * 64

    for pair in range(SLOTS // 2):
        two = [facts(*PIECES[2 * pair + j]) for j in range(2)]
        for r in range(CELLS):
            vals = []
            for j, (kb, base) in enumerate(two):
                see = (kb < blocks - CELLS + r) & (pattern_ref[r, kb] == 1)
                same = kb == blocks - CELLS + r
                const = jnp.where(see, -BLOCK, jnp.where(same, base - j * PER, 4 * BLOCK))
                vals.append(const + lane * jnp.where(same, 1, 0))
            row = jnp.where(lane < PER, vals[0], vals[1]).astype(jnp.float32)
            o_ref[r : r + 1, pair * 128 : (pair + 1) * 128] = row


def thresholds(pattern, stripe):
    return pl.pallas_call(
        threshold_kernel,
        out_shape=jax.ShapeDtypeStruct((CELLS, KEYS), jnp.float32),
        in_specs=[pl.BlockSpec(memory_space=pltpu.SMEM)] * 2,
        compiler_params=SMALL,
        cost_estimate=pl.CostEstimate(flops=50_000_000_000, bytes_accessed=100_000, transcendentals=0),
        name="thresholds",
    )(pattern, stripe)


def body(queries, latents, key_rope, key_up, value_up, pattern, stripe):
    cells = ("xl", "y")
    groups = ("xh", "z")
    def swap(after):
        send = queries.reshape(TOK, GRP, HEADS * QD).transpose(1, 0, 2)
        send, _ = lax.optimization_barrier((send, after))
        return lax.all_to_all(send, groups, split_axis=0, concat_axis=0, tiled=True)

    def prepare(after):
        up, down, seen, order, _ = lax.optimization_barrier(
            (key_up, value_up, pattern, stripe, after)
        )
        weights = jnp.concatenate([up.transpose(0, 2, 1), down], axis=2)
        return weights, thresholds(seen, order)

    got, to_core, mine, (weights, thr) = gather_keys(latents, key_rope, swap, prepare)
    mine = mine.reshape(GRP * TOK, HEADS * QD)
    send = jnp.broadcast_to(mine[None], (CELLS, *mine.shape))
    q = lax.all_to_all(send, cells, split_axis=0, concat_axis=0, tiled=True)
    q = q.reshape(ROWS, HEADS * QD)
    before = attend([got[c] for c in EARLY], q, weights, thr)
    (got[0, 3], got[0, 4]), before = lax.optimization_barrier(((got[0, 3], got[0, 4]), before))
    for s in (3, 4):
        got[1, s] = to_core(got[0, s])
    part = attend([got[c] for c in LATE], q, weights, thr, before)
    back = lax.all_to_all(
        part.reshape(CELLS, GRP * TOK, EXT), cells, split_axis=0, concat_axis=0, tiled=True
    )
    out = lax.all_to_all(combine(back.reshape(ROWS, EXT)), groups, split_axis=0, concat_axis=0, tiled=True)
    return out.transpose(1, 0, 2).reshape(TOK, GRP * MSG)


def solution(mesh):
    fine = Mesh(mesh.devices.reshape(XLN, YN, CN, XHN, ZN), AXES)
    in_specs = (
        P(AXES, None),
        P(AXES, None),
        P(AXES, None),
        P(("xh", "z"), None, None),
        P(("xh", "z"), None, None),
        P(),
        P(),
    )
    return jax.shard_map(body, mesh=fine, in_specs=in_specs, out_specs=P(AXES, None), check_vma=False)
```

```python
import functools
import math

import jax
import jax.numpy as jnp
from jax import lax
from jax.experimental import pallas as pl
from jax.experimental.pallas import tpu as pltpu
from jax.sharding import Mesh
from jax.sharding import PartitionSpec as P

L = 512
QN = 128
QR = 64
QD = QN + QR
VD = 128
BLOCK = 128
HEADS = 4
NEG = -1e30
SCALE = 1.0 / math.sqrt(QD)
LOG2E = math.log2(math.e)

AXES = ("xl", "y", "core", "xh", "z")
XLN, YN, CN, XHN, ZN = 2, 4, 2, 2, 8
CELLS = XLN * YN
GRP = XHN * ZN
PER = 64
TOK = 4
ROWS = CELLS * GRP * TOK
MSG = HEADS * VD
EXT = MSG + 128

HALF = 80
FOUR = 4 * PER
FULL = FOUR + 32

EARLY = [(0, 0)] + [(o, s) for s in (1, 2) for o in (0, 1)]
LATE = [(0, 3), (1, 3), (0, 4), (1, 4)]
PIECES = [(j % 2, o, s, j // 2) for o, s in EARLY + LATE for j in range(4 if s < 4 else 2)]
SLOTS = len(PIECES)
KEYS = SLOTS * PER

VAT = 256
QT = 256
KT = FOUR
SMALL = pltpu.CompilerParams(vmem_limit_bytes=8 * 1024 * 1024)


def attend_kernel(count, first, *refs):
    if first:
        chunks, halves, refs = refs[: count - 1], refs[count - 1 : count + 1], refs[count + 1 :]
        q_ref, w_ref, thr_ref, old_ref, lse_ref, o_ref, kv, sco, pair = refs
        for j, ref in enumerate(halves):
            pair[j * 2 * PER : (j + 1) * 2 * PER, :] = ref[0 : 2 * PER, :]
            pair[FOUR + j * 16 : FOUR + (j + 1) * 16, :] = ref[2 * PER :, :]
        chunks = (*chunks, pair)
    else:
        chunks, refs = refs[:count], refs[count:]
        q_ref, w_ref, thr_ref, o_ref, lse_ref, kv, sco = refs
    units = [(h, t) for h in range(HEADS) for t in range(ROWS // QT)]
    off = lax.broadcasted_iota(jnp.int32, (64, 128), 0).astype(jnp.float32)
    lane = lax.broadcasted_iota(jnp.int32, (QT, 128), 1)

    def project(h, c):
        new = jnp.dot(chunks[c][0:FOUR, :], w_ref[h], preferred_element_type=jnp.float32)
        new = new.astype(jnp.bfloat16)
        rows = slice(c * FOUR, (c + 1) * FOUR)
        kv[h % 2, rows, 0:QN] = new[:, 0:QN]
        kv[h % 2, rows, VAT:] = new[:, QN:]

    for c in range(count):
        for r in range(FOUR // 16):
            at = FOUR + 16 * (r // 8)
            rope = chunks[c][at : at + 16, (r % 8) * QR : (r % 8 + 1) * QR]
            for b in range(2):
                kv[b, c * FOUR + r * 16 : c * FOUR + (r + 1) * 16, QN:QD] = rope
        project(0, c)

    def score(u, i, top):
        h, t = units[u]
        q = q_ref[t * QT : (t + 1) * QT, h * QD : (h + 1) * QD]
        s = lax.dot_general(
            q,
            kv[h % 2, i * KT : (i + 1) * KT, 0:QD],
            (((1,), (1,)), ((), ())),
            preferred_element_type=jnp.float32,
        )
        parts = []
        for b in range(QT // 64):
            row = t * (QT // 64) + b
            at = (first + i) * KT
            thr = thr_ref[row : row + 1, at : at + KT]
            cols = []
            for c in range(KT // 128):
                piece = s[b * 64 : (b + 1) * 64, c * 128 : (c + 1) * 128]
                cols.append(jnp.where(off >= thr[:, c * 128 : (c + 1) * 128], piece, NEG))
            parts.append(functools.reduce(jnp.maximum, cols))
            for c in range(KT // 128):
                at = i * KT + c * 128
                sco[u % 2, b * 64 : (b + 1) * 64, at : at + 128] = cols[c]
        best = jnp.concatenate(parts, axis=0)
        return best if top is None else jnp.maximum(top, best)

    def mix(u, i, mc, total, acc):
        h, t = units[u]
        p = jnp.exp2(sco[u % 2, :, i * KT : (i + 1) * KT] * (SCALE * LOG2E) - mc)
        for c in range(KT // 128):
            piece = p[:, c * 128 : (c + 1) * 128]
            total = piece if total is None else total + piece
        new = jnp.dot(
            p.astype(jnp.bfloat16),
            kv[h % 2, i * KT : (i + 1) * KT, VAT:],
            preferred_element_type=jnp.float32,
        )
        return total, new if acc is None else acc + new

    stats = [jnp.zeros((QT, 128), jnp.float32) for _ in range(ROWS // QT)]
    m = None
    for u in range(len(units) + 1):
        top = total = acc = None
        if u:
            mc = m * (SCALE * LOG2E)
        for i in range(count):
            if u < len(units):
                top = score(u, i, top)
            if u:
                total, acc = mix(u - 1, i, mc, total, acc)
            if u < len(units):
                h, t = units[u]
                if t == ROWS // QT - 1 and h + 1 < HEADS:
                    project(h + 1, i)
        if u:
            h, t = units[u - 1]
            rows = slice(t * QT, (t + 1) * QT)
            den = jnp.sum(total, axis=1, keepdims=True)
            lse = m * SCALE + jnp.log(den)
            out = acc / den
            cols = slice(h * VD, (h + 1) * VD)
            if first:
                before = lse_ref[rows, h : h + 1]
                both = jnp.maximum(before, lse)
                part, rest = jnp.exp(lse - both), jnp.exp(before - both)
                out = (out * part + old_ref[rows, cols] * rest) / (part + rest)
                lse = both + jnp.log(part + rest)
                hi = lse.astype(jnp.bfloat16).astype(jnp.float32)
                mid = (lse - hi).astype(jnp.bfloat16).astype(jnp.float32)
                old = jnp.where(lane == 3 * h, hi, stats[t])
                old = jnp.where(lane == 3 * h + 1, mid, old)
                stats[t] = jnp.where(lane == 3 * h + 2, lse - hi - mid, old)
            else:
                stats[t] = jnp.where(lane == h, lse, stats[t])
            o_ref[rows, cols] = out.astype(o_ref.dtype)
        if u < len(units):
            m = jnp.max(top, axis=1, keepdims=True)
    for t in range(ROWS // QT):
        if first:
            o_ref[t * QT : (t + 1) * QT, MSG:] = stats[t].astype(jnp.bfloat16)
        else:
            lse_ref[t * QT : (t + 1) * QT, :] = stats[t]


def attend(chunks, q, weights, thr, before=()):
    count = len(chunks) - 1 if before else len(chunks)
    first = len(EARLY) if before else 0
    scratch = [
        pltpu.VMEM((2, count * FOUR, VAT + VD), jnp.bfloat16),
        pltpu.VMEM((2, QT, count * FOUR), jnp.float32),
    ]
    if before:
        scratch.append(pltpu.VMEM((FULL, L), jnp.bfloat16))
        shape = jax.ShapeDtypeStruct((ROWS, EXT), jnp.bfloat16)
    else:
        shape = (
            jax.ShapeDtypeStruct((ROWS, MSG), jnp.float32),
            jax.ShapeDtypeStruct((ROWS, 128), jnp.float32),
        )
    return pl.pallas_call(
        functools.partial(attend_kernel, count, first),
        out_shape=shape,
        scratch_shapes=scratch,
        compiler_params=pltpu.CompilerParams(vmem_limit_bytes=24 * 1024 * 1024),
        cost_estimate=pl.CostEstimate(
            flops=1_000_000 * count, bytes_accessed=1_000 * count, transcendentals=1_000 * count
        ),
        name="attend_late" if before else "attend_early",
    )(*chunks, q, weights, thr, *before)


def combine_kernel(x_ref, o_ref):
    n = GRP * TOK
    ext = [x_ref[pl.ds(c * n, n), MSG:].astype(jnp.float32) for c in range(CELLS)]
    for h in range(HEADS):
        j = 3 * h
        lse = [e[:, j : j + 1] + e[:, j + 1 : j + 2] + e[:, j + 2 : j + 3] for e in ext]
        top = functools.reduce(jnp.maximum, lse)
        part = [jnp.exp(v - top) for v in lse]
        scale = 1.0 / functools.reduce(jnp.add, part)
        acc = jnp.zeros((n, VD), jnp.float32)
        for c in range(CELLS):
            acc = acc + x_ref[pl.ds(c * n, n), pl.ds(h * VD, VD)].astype(jnp.float32) * (
                part[c] * scale
            )
        o_ref[:, :, pl.ds(h * VD, VD)] = acc.reshape(GRP, TOK, VD).astype(jnp.bfloat16)


def combine(x):
    return pl.pallas_call(
        combine_kernel,
        out_shape=jax.ShapeDtypeStruct((GRP, TOK, MSG), jnp.bfloat16),
        compiler_params=SMALL,
        name="combine",
    )(x)


def pack_kernel(lat_ref, rope_ref, o_ref):
    o_ref[0:PER, :] = lat_ref[...]
    for r in range(L // QR):
        b = r % (PER // 16)
        o_ref[PER:HALF, r * QR : (r + 1) * QR] = rope_ref[b * 16 : (b + 1) * 16, :]


def pack(latents, key_rope):
    return pl.pallas_call(
        pack_kernel,
        out_shape=jax.ShapeDtypeStruct((HALF, L), jnp.bfloat16),
        compiler_params=SMALL,
        name="pack",
    )(latents, key_rope)


def merge_kernel(*refs):
    o_ref = refs[-1]
    for j, ref in enumerate(refs[:-1]):
        half = slice(j % 2 * (L // 2), (j % 2 + 1) * (L // 2))
        at = FOUR + j // 2 * 16
        o_ref[j * PER : (j + 1) * PER, :] = ref[0:PER, :]
        o_ref[at : at + 16, half] = ref[PER:HALF, half]


def merge(pieces):
    return pl.pallas_call(
        merge_kernel,
        out_shape=jax.ShapeDtypeStruct((FULL, L), jnp.bfloat16),
        compiler_params=SMALL,
        name="merge",
    )(*pieces)


def halve_kernel(x_ref, o_ref):
    o_ref[0 : 2 * PER, :] = x_ref[0 : 2 * PER, :]
    o_ref[2 * PER :, :] = x_ref[FOUR : FOUR + 16, :]


def halve(chunk):
    return pl.pallas_call(
        halve_kernel,
        out_shape=jax.ShapeDtypeStruct((FULL // 2, L), jnp.bfloat16),
        compiler_params=SMALL,
        name="halve",
    )(chunk)


def shift(n, k):
    return [(i, (i + k) % n) for i in range(n)]


def gather_keys(latents, key_rope, swap, prepare):
    near = [(a * 2 + b, (1 - a) * 2 + 1 - b) for a in range(2) for b in range(2)]
    to_core = lambda x: lax.ppermute(x, "core", shift(CN, 1))

    def round_z(x, n):
        up = [(i, (i + n) % ZN) for i in range(ZN)]
        down = [(ZN + i, ZN + (i - n) % ZN) for i in range(ZN)]
        return lax.ppermute(x, ("core", "z"), up + down)

    piece = pack(latents, key_rope)
    beside, mate = lax.ppermute(piece, ("xl", "xh"), near), to_core(piece)
    mine = swap()
    pieces = [piece, beside, mate, to_core(beside)]
    pieces, mine = lax.optimization_barrier((pieces, mine))
    now = merge(pieces)
    got = {(0, 0): now, (0, 1): round_z(now, 1), (0, 2): round_z(now, 2)}
    got[0, 2], extra = lax.optimization_barrier((got[0, 2], prepare(beside)))
    got[0, 3] = round_z(got[0, 2], 1)
    got[0, 4] = round_z(halve(got[0, 2]), 2)
    for s in (1, 2):
        got[1, s] = to_core(got[0, s])
    mine, _ = lax.optimization_barrier((mine, now))
    return got, to_core, mine, extra


def threshold_kernel(pattern_ref, stripe_ref, o_ref):
    xl, y, core = lax.axis_index("xl"), lax.axis_index("y"), lax.axis_index("core")
    xh, z = lax.axis_index("xh"), lax.axis_index("z")
    lane = lax.broadcasted_iota(jnp.int32, (1, 128), 1)
    blocks = stripe_ref.shape[0]

    def facts(swap, other, step, inner):
        side = core ^ other
        zz = lax.rem(z + jnp.where(side == 1, step, ZN - step), ZN)
        cell = ((xl ^ swap) * YN + y) * CN + (side ^ inner)
        place = cell * GRP + (xh ^ swap) * ZN + zz
        return stripe_ref[lax.shift_right_logical(place, 1)], (place & 1) * PER - core * 64

    for pair in range(SLOTS // 2):
        two = [facts(*PIECES[2 * pair + j]) for j in range(2)]
        for r in range(CELLS):
            vals = []
            for j, (kb, base) in enumerate(two):
                see = (kb < blocks - CELLS + r) & (pattern_ref[r, kb] == 1)
                same = kb == blocks - CELLS + r
                const = jnp.where(see, -BLOCK, jnp.where(same, base - j * PER, 4 * BLOCK))
                vals.append(const + lane * jnp.where(same, 1, 0))
            row = jnp.where(lane < PER, vals[0], vals[1]).astype(jnp.float32)
            o_ref[r : r + 1, pair * 128 : (pair + 1) * 128] = row


def thresholds(pattern, stripe):
    return pl.pallas_call(
        threshold_kernel,
        out_shape=jax.ShapeDtypeStruct((CELLS, KEYS), jnp.float32),
        in_specs=[pl.BlockSpec(memory_space=pltpu.SMEM)] * 2,
        compiler_params=SMALL,
        cost_estimate=pl.CostEstimate(flops=50_000_000_000, bytes_accessed=100_000, transcendentals=0),
        name="thresholds",
    )(pattern, stripe)


def body(queries, latents, key_rope, key_up, value_up, pattern, stripe):
    cells = ("xl", "y")
    groups = ("xh", "z")
    def swap():
        send = queries.reshape(TOK, GRP, HEADS * QD).transpose(1, 0, 2)
        return lax.all_to_all(send, groups, split_axis=0, concat_axis=0, tiled=True)

    def prepare(after):
        up, down, seen, order, _ = lax.optimization_barrier(
            (key_up, value_up, pattern, stripe, after)
        )
        weights = jnp.concatenate([up.transpose(0, 2, 1), down], axis=2)
        return weights, thresholds(seen, order)

    got, to_core, mine, (weights, thr) = gather_keys(latents, key_rope, swap, prepare)
    mine = mine.reshape(GRP * TOK, HEADS * QD)
    send = jnp.broadcast_to(mine[None], (CELLS, *mine.shape))
    q = lax.all_to_all(send, cells, split_axis=0, concat_axis=0, tiled=True)
    q = q.reshape(ROWS, HEADS * QD)
    before = attend([got[c] for c in EARLY], q, weights, thr)
    (got[0, 3], got[0, 4]), before = lax.optimization_barrier(((got[0, 3], got[0, 4]), before))
    for s in (3, 4):
        got[1, s] = to_core(got[0, s])
    part = attend([got[c] for c in LATE], q, weights, thr, before)
    back = lax.all_to_all(
        part.reshape(CELLS, GRP * TOK, EXT), cells, split_axis=0, concat_axis=0, tiled=True
    )
    out = lax.all_to_all(combine(back.reshape(ROWS, EXT)), groups, split_axis=0, concat_axis=0, tiled=True)
    return out.transpose(1, 0, 2).reshape(TOK, GRP * MSG)


def solution(mesh):
    fine = Mesh(mesh.devices.reshape(XLN, YN, CN, XHN, ZN), AXES)
    in_specs = (
        P(AXES, None),
        P(AXES, None),
        P(AXES, None),
        P(("xh", "z"), None, None),
        P(("xh", "z"), None, None),
        P(),
        P(),
    )
    return jax.shard_map(body, mesh=fine, in_specs=in_specs, out_specs=P(AXES, None), check_vma=False)
```
